768 devices in a mesh: dp: 24 (over y_lo, z), fsdp: 32 (over y_hi, x, core).
Axes of the slice: x: 4, y: 8 (y_hi: 4, y_lo: 2; y = y_hi * 2 + y_lo), z: 12, core: 2. Of those that a mesh axis runs over, the one named last changes fastest.
Arguments:
- rollout: bfloat16 [147456, 2048], P(('dp', 'fsdp')), may hold values from -6 to 6
- flows: int32 [24, 32], P(None, 'fsdp'), may hold values from -32 to 32, as said below
- route_ids: int32 [98304, 8], P(('dp', 'fsdp')), may hold values from 0 to 127, all different within a row; in each aligned block of 128 rows (0 to 127, 128 to 255, ...) at most 12 rows name the same one
- route_logits: float32 [98304, 8], P(('dp', 'fsdp')), may hold values from -18 to 406
- grad_out: bfloat16 [98304, 2048], P(('dp', 'fsdp')), may hold values from -0.099609375 to 0.099609375
- w_gate: bfloat16 [32, 2048, 768], P('fsdp'), may hold values from -0.125 to 0.125
- w_up: bfloat16 [32, 2048, 768], P('fsdp'), may hold values from -0.125 to 0.125
- w_down: bfloat16 [32, 768, 2048], P('fsdp'), may hold values from -0.21875 to 0.21875
Outputs:
- moe_out: bfloat16 [98304, 2048], P(('dp', 'fsdp'))
- router_grad: float32 [128, 2048], P('fsdp')
The draws below stay inside these ranges and needn't reach their ends.
Inputs may be any that keep to these rules, and one draw needn't show every extreme that they name: `route_ids`: each row names 8 different experts; in the rows of one device (aligned blocks of 128 rows) no expert is named more than 12 times. flows[r, j] live tokens pass from data rank r to rank (r + 1) mod 24 in fsdp column j; a negative entry passes -flows[r, j] tokens from rank (r + 1) mod 24 to rank r. Both 32 and -32 occur.
All inputs are finite; a program needn't handle non-finite values.
Results may differ from the reference program's by a relative error of at most 0.0057.
Values may be sent and summed in bfloat16 or wider, within the bound.
No kernel may reach another device: no remote copies, remote signals or barrier semaphores. Data moves between devices by JAX's collectives and lax.ppermute only.
A program may use at most 64 MiB of HBM per device.

```python
import math
import jax
import jax.numpy as jnp
import numpy as np
from jax import lax

D = 2048
FF = 768
EXPERTS = 128
TOPK = 8
TOK_DEV = 128
MOVE = 32
SRC_DEV = 192
CAP = 12
WIN = 32
TOKENS = 98304
SRC_ROWS = 147456
N_DP = 24
N_FSDP = 32


def draw_flows(key, part):
    key = jax.random.fold_in(key, 11)
    base_key, first_key, second_key = jax.random.split(key, 3)
    total_cells = N_DP * N_FSDP
    values = jax.random.randint(base_key, (N_DP, N_FSDP), 0 - MOVE, MOVE + 1, jnp.int32)
    first_spot = jax.random.randint(first_key, (), 0, total_cells, jnp.int32)
    second_spot = (first_spot + 1 + jax.random.randint(second_key, (), 0, total_cells - 1, jnp.int32)) % total_cells
    positions = jnp.arange(total_cells, dtype=jnp.int32).reshape(N_DP, N_FSDP)
    values = jnp.where(positions == first_spot, MOVE, values)
    values = jnp.where(positions == second_spot, 0 - MOVE, values)
    return values


def draw_route_logits(key, part):
    key = jax.random.fold_in(key, 7)
    base_key = jax.random.fold_in(key, 0)
    values = jnp.clip(3.0 * jax.random.normal(base_key, (TOKENS, TOPK), jnp.float32), -18.0, 18.0)
    return values


def block_levels(key, extent, cuts, low, high):
    level, own = 1.0, jax.random.fold_in(key, 6)
    for axis_at, shards_of in cuts:
        draws = jnp.exp(jax.random.uniform(jax.random.fold_in(own, axis_at), (shards_of,), jnp.float32, low / len(cuts), high / len(cuts)))
        level = level * jnp.repeat(draws, extent[axis_at] // shards_of).reshape([-1 if axis == axis_at else 1 for axis in range(len(extent))])
    return level


def deal_out(stream_key, own, number, rows, number_of, top, reach, slope):
    sequence = jax.random.permutation(stream_key, number_of)
    heavy_load, common = load_shares(number_of, rows * top, reach, slope, True), load_shares(number_of, rows * top, reach, slope, False)
    places = jnp.arange(number_of)

    def named(lengths, offset_by):
        used = int((lengths > 0).sum())
        fixed = max(1, used // 4)
        moved = fixed + (places - fixed + offset_by * (used - fixed)) % max(1, number_of - fixed)
        return jnp.zeros((number_of,), jnp.int32).at[sequence[jnp.where(places < fixed, places, moved)]].set(jnp.asarray(lengths, jnp.int32))

    lengths = jnp.where(number % 4 == 0, named(heavy_load, number // 4), named(common, number - number // 4 - 1))
    mixed = jax.random.permutation(jax.random.fold_in(own, 3), number_of)
    giver, sink = mixed[0:number_of // 2 * 2:2], mixed[1:number_of // 2 * 2:2]
    margin = jnp.minimum(lengths[giver] - 1, reach - lengths[sink]) // 2
    margin = jnp.where((giver == sequence[0]) | (sink == sequence[0]) | (lengths[sink] == 0), 0, jnp.maximum(margin, 0))
    moved = jax.random.randint(jax.random.fold_in(own, 4), (number_of // 2,), 0, 1 << 20) % (margin + 1)
    lengths = lengths.at[giver].add(-moved).at[sink].add(moved)
    items = jnp.searchsorted(jnp.cumsum(lengths), jnp.arange(rows * top), side="right").astype(jnp.int32)
    grid = items.reshape(top, rows).T
    grid = grid[jax.random.permutation(jax.random.fold_in(own, 1), rows)]
    offset_by = jax.random.randint(jax.random.fold_in(own, 2), (rows, 1), 0, top)
    return jnp.take_along_axis(grid, (jnp.arange(top)[None, :] + offset_by) % top, axis=1)


def load_shares(number_of, total, reach, skew, full):
    weights = [(1 << 20) // math.isqrt(grade ** skew) + 1 for grade in range(1, number_of + 1)]
    largest = reach if full else min(reach, max(-(-total // number_of), total * weights[0] // sum(weights)))
    least = 1 if total - largest >= number_of - 1 else 0
    holding, spare = [largest] + [least] * (number_of - 1), total - largest - least * (number_of - 1)
    while spare > 0:
        candidates = [i for i in range(1, number_of) if holding[i] < largest] or [i for i in range(1, number_of) if holding[i] < reach]
        pool, budget = sum([weights[i] for i in candidates]), spare
        for i in candidates:
            addition = min(reach - holding[i], max(1, budget * weights[i] // pool), spare)
            holding[i] = holding[i] + addition
            spare = spare - addition
    return np.array(holding)


def normal_values(stream_key, dims, scale, most, pieces=(), kind=jnp.bfloat16):
    level = block_levels(stream_key, dims, pieces, -0.22, 0.18) if pieces else 1.0
    values = jax.random.normal(stream_key, dims, jnp.float32) * scale * level
    return jnp.minimum(jnp.maximum(values, -most), most).astype(kind)


def setup_inputs(seed: int = 0) -> dict:
    splits = jax.random.split(jax.random.key(seed), 9)
    rollout = normal_values(splits[0], (SRC_ROWS, D), 1.0, 6.0, ((0, 768),))
    flows = draw_flows(jax.random.fold_in(splits[8], 71), 0)
    route_ids_keys = jax.random.split(jax.random.fold_in(splits[2], 1), TOKENS // TOK_DEV)
    route_ids_turns = jax.random.permutation(jax.random.fold_in(splits[2], 3), TOKENS // TOK_DEV)
    route_ids = jax.vmap(lambda own, number: deal_out(jax.random.fold_in(splits[2], 2), own, number, TOK_DEV, EXPERTS, TOPK, CAP, 2))(route_ids_keys, route_ids_turns).reshape((TOKENS, TOPK))
    route_logits = draw_route_logits(jax.random.fold_in(splits[8], 71), 0)
    grad_out = normal_values(splits[4], (TOKENS, D), 0.015625, 0.099609375, ((0, 768),))
    w_gate = normal_values(splits[5], (WIN, D, FF), D ** -0.5, 0.125, ((0, 32),))
    w_up = normal_values(splits[6], (WIN, D, FF), D ** -0.5, 0.125, ((0, 32),))
    w_down = normal_values(splits[7], (WIN, FF, D), FF ** -0.5, 0.21875, ((0, 32),))
    return {"rollout": rollout, "flows": flows, "route_ids": route_ids, "route_logits": route_logits, "grad_out": grad_out, "w_gate": w_gate, "w_up": w_up, "w_down": w_down}


def arrange(chosen, experts_here):
    member = chosen[:, :, None] == jnp.arange(experts_here, dtype=jnp.int32)[None, None, :]
    picked = jnp.any(member, axis=1).astype(jnp.int32)
    slot_order = jnp.cumsum(picked, axis=0, dtype=jnp.int32) - 1
    slot_place = (picked[:, :, None] == 1) & (slot_order[:, :, None] == jnp.arange(CAP, dtype=jnp.int32)[None, None, :])
    return slot_order, slot_place


def dispatch_rows(token_block, chosen, experts_here):
    slot_place = arrange(chosen, experts_here)[1]
    place_matrix = slot_place.reshape(TOK_DEV, experts_here * CAP).astype(jnp.bfloat16)
    gathered = jnp.dot(place_matrix.T, token_block, preferred_element_type=jnp.float32)
    return gathered.astype(jnp.bfloat16).reshape(experts_here, CAP, D)


def expert_apply(slot_rows, gate_matrix, up_matrix, down_matrix):
    gate_act = jnp.dot(slot_rows, gate_matrix, preferred_element_type=jnp.float32)
    up_act = jnp.dot(slot_rows, up_matrix, preferred_element_type=jnp.float32)
    hidden = (jax.nn.silu(gate_act) * up_act).astype(jnp.bfloat16)
    return jnp.dot(hidden, down_matrix, preferred_element_type=jnp.float32).astype(jnp.bfloat16)


def combine(token_block, chosen, logits, cotangent, returned, experts_here):
    slot_order = arrange(chosen, experts_here)[0]
    route_weight = jax.nn.softmax(logits, axis=1)
    clamped = jnp.minimum(chosen, experts_here - 1)
    order_at = jnp.take_along_axis(slot_order, clamped, axis=1)
    inside = chosen < experts_here
    slot_count = experts_here * CAP
    flat_index = jnp.where(inside, clamped * CAP + order_at, slot_count)
    slot_table = returned.reshape(slot_count, D)
    columns = jnp.arange(slot_count, dtype=jnp.int32)
    pick = (flat_index[:, :, None] == columns[None, None, :]).astype(jnp.float32)
    weight_matrix = jnp.sum(route_weight[:, :, None] * pick, axis=1)
    layer_out = jnp.dot(weight_matrix, slot_table.astype(jnp.float32), precision=lax.Precision.HIGHEST).astype(jnp.bfloat16)
    slot_scores = jnp.dot(cotangent, slot_table.T, preferred_element_type=jnp.float32)
    slot_scores = jnp.concatenate([slot_scores, jnp.zeros((slot_scores.shape[0], 1), jnp.float32)], axis=1)
    scores = jnp.take_along_axis(slot_scores, flat_index, axis=1)
    logit_grad = route_weight * (scores - jnp.sum(route_weight * scores, axis=1, keepdims=True))
    one_hot = (chosen[:, :, None] == jnp.arange(EXPERTS, dtype=jnp.int32)[None, None, :]).astype(jnp.float32)
    expert_grad = jnp.sum(logit_grad[:, :, None] * one_hot, axis=1)
    router_term = jnp.dot(expert_grad.T, token_block.astype(jnp.float32), precision=lax.Precision.HIGHEST)
    return layer_out, router_term


def settle(held, left_edge, right_edge, live_count, left_flow):
    sectioning = jnp.concatenate([left_edge, held, jnp.zeros((MOVE, D), jnp.bfloat16)], axis=0)
    sectioning = lax.dynamic_update_slice_in_dim(sectioning, right_edge, MOVE + live_count, 0)
    return lax.dynamic_slice_in_dim(sectioning, MOVE - left_flow, TOK_DEV, 0)


def tail_window(token_block, live_count):
    return lax.dynamic_slice_in_dim(token_block, live_count - MOVE, MOVE, 0)


def reference(rollout, flows, route_ids, route_logits, grad_out, w_gate, w_up, w_down):
    devices = N_DP * N_FSDP
    held = rollout.reshape(N_DP, N_FSDP, SRC_DEV, D)
    left_flows = jnp.roll(flows, 1, axis=0)
    live_counts = TOK_DEV + flows - left_flows
    head_rows = held[:, :, :MOVE]
    tails = jax.vmap(jax.vmap(tail_window))(held, live_counts)
    from_left = jnp.roll(tails, 1, axis=0)
    from_right = jnp.roll(head_rows, -1, axis=0)
    balanced = jax.vmap(jax.vmap(settle))(held, from_left, from_right, live_counts, left_flows)
    balanced = balanced.reshape(devices, TOK_DEV, D)
    chosen = route_ids.reshape(devices, TOK_DEV, TOPK)
    logits = route_logits.reshape(devices, TOK_DEV, TOPK)
    cotangent = grad_out.reshape(devices, TOK_DEV, D)

    def outgoing_of(inputs_now):
        return dispatch_rows(inputs_now[0], inputs_now[1], N_FSDP)

    outgoing = lax.map(outgoing_of, (balanced, chosen))

    def expert_of(inputs_now):
        expert_index, gate_matrix, up_matrix, down_matrix = inputs_now
        slot_rows = lax.dynamic_index_in_dim(outgoing, expert_index, axis=1, keepdims=False)
        computed = expert_apply(slot_rows.reshape(devices * CAP, D), gate_matrix, up_matrix, down_matrix)
        return computed.reshape(devices, CAP, D)

    results = lax.map(expert_of, (jnp.arange(N_FSDP, dtype=jnp.int32), w_gate, w_up, w_down))

    def settle_device(summed, inputs_now):
        token_block, block_ids, block_logits, block_cot, device_index = inputs_now
        returned = lax.dynamic_index_in_dim(results, device_index, axis=1, keepdims=False)
        layer_out, router_term = combine(token_block, block_ids, block_logits, block_cot, returned, N_FSDP)
        return summed + router_term, layer_out

    summed, layer_out = lax.scan(settle_device, jnp.zeros((EXPERTS, D), jnp.float32), (balanced, chosen, logits, cotangent, jnp.arange(devices, dtype=jnp.int32)))
    return layer_out.reshape(TOKENS, D), summed
```

```python
import jax
import jax.numpy as jnp
from jax import lax
from jax.sharding import Mesh
from jax.sharding import PartitionSpec as P

D = 2048
EXPERTS = 128
TOK_DEV = 128
MOVE = 32
CAP = 12
DP = ("yl", "z")


def extended(cells, sides, width):
    for axis, dim in sides:
        count = lax.axis_size(axis)
        head = lax.slice_in_dim(cells, 0, width, axis=dim)
        tail = lax.slice_in_dim(cells, cells.shape[dim] - width, cells.shape[dim], axis=dim)
        cells = jnp.concatenate(
            [
                lax.ppermute(tail, axis, [(i, (i + 1) % count) for i in range(count)]),
                cells,
                lax.ppermute(head, axis, [((i + 1) % count, i) for i in range(count)]),
            ],
            axis=dim,
        )
    return cells


def arrange(chosen, experts_here):
    member = chosen[:, :, None] == jnp.arange(experts_here, dtype=jnp.int32)[None, None, :]
    picked = jnp.any(member, axis=1).astype(jnp.int32)
    slot_order = jnp.cumsum(picked, axis=0, dtype=jnp.int32) - 1
    slot_place = (picked[:, :, None] == 1) & (
        slot_order[:, :, None] == jnp.arange(CAP, dtype=jnp.int32)[None, None, :]
    )
    return (slot_order, slot_place)


def dispatch_rows(token_block, chosen, experts_here):
    slot_place = arrange(chosen, experts_here)[1]
    place_matrix = slot_place.reshape(TOK_DEV, experts_here * CAP).astype(jnp.bfloat16)
    gathered = jnp.dot(place_matrix.T, token_block, preferred_element_type=jnp.float32)
    return gathered.astype(jnp.bfloat16).reshape(experts_here, CAP, D)


def expert_apply(slot_rows, gate_matrix, up_matrix, down_matrix):
    gate_act = jnp.dot(slot_rows, gate_matrix, preferred_element_type=jnp.float32)
    up_act = jnp.dot(slot_rows, up_matrix, preferred_element_type=jnp.float32)
    hidden = (jax.nn.silu(gate_act) * up_act).astype(jnp.bfloat16)
    return jnp.dot(hidden, down_matrix, preferred_element_type=jnp.float32).astype(jnp.bfloat16)


def combine(token_block, chosen, logits, cotangent, returned, experts_here):
    slot_order = arrange(chosen, experts_here)[0]
    route_weight = jax.nn.softmax(logits, axis=1)
    clamped = jnp.minimum(chosen, experts_here - 1)
    order_at = jnp.take_along_axis(slot_order, clamped, axis=1)
    inside = chosen < experts_here
    slot_count = experts_here * CAP
    flat_index = jnp.where(inside, clamped * CAP + order_at, slot_count)
    slot_table = returned.reshape(slot_count, D)
    columns = jnp.arange(slot_count, dtype=jnp.int32)
    pick = (flat_index[:, :, None] == columns[None, None, :]).astype(jnp.float32)
    weight_matrix = jnp.sum(route_weight[:, :, None] * pick, axis=1)
    layer_out = jnp.dot(
        weight_matrix, slot_table.astype(jnp.float32), precision=lax.Precision.HIGHEST
    ).astype(jnp.bfloat16)
    slot_scores = jnp.dot(cotangent, slot_table.T, preferred_element_type=jnp.float32)
    slot_scores = jnp.concatenate(
        [slot_scores, jnp.zeros((slot_scores.shape[0], 1), jnp.float32)], axis=1
    )
    scores = jnp.take_along_axis(slot_scores, flat_index, axis=1)
    logit_grad = route_weight * (scores - jnp.sum(route_weight * scores, axis=1, keepdims=True))
    one_hot = (chosen[:, :, None] == jnp.arange(EXPERTS, dtype=jnp.int32)[None, None, :]).astype(
        jnp.float32
    )
    expert_grad = jnp.sum(logit_grad[:, :, None] * one_hot, axis=1)
    router_term = jnp.dot(
        expert_grad.T, token_block.astype(jnp.float32), precision=lax.Precision.HIGHEST
    )
    return (layer_out, router_term)


def settle(held, left_edge, right_edge, live_count, left_flow):
    sectioning = jnp.concatenate([left_edge, held, jnp.zeros((MOVE, D), jnp.bfloat16)], axis=0)
    sectioning = lax.dynamic_update_slice_in_dim(sectioning, right_edge, MOVE + live_count, 0)
    return lax.dynamic_slice_in_dim(sectioning, MOVE - left_flow, TOK_DEV, 0)


def exchange(blocks, axes):
    return lax.all_to_all(blocks, axes, split_axis=0, concat_axis=0, tiled=True)


def router_sum(router_term):
    blocks = router_term.reshape(32, 4, 2, 2, 512).transpose(2, 0, 3, 1, 4).reshape(64, 8, 512)
    terms = exchange(blocks.astype(jnp.bfloat16), ("yl", "fsdp"))
    part = jnp.sum(terms.astype(jnp.float32), axis=0).astype(jnp.bfloat16)
    parts = exchange(jnp.broadcast_to(part[None], (24, 8, 512)), ("yl", "z"))
    halves = jnp.sum(parts.astype(jnp.float32).reshape(2, 12, 2, 4, 512), axis=1)
    return halves.transpose(2, 0, 1, 3).reshape(4, D)


def shards(rollout, flows, route_ids, route_logits, grad_out, w_gate, w_up, w_down):
    data_rank = lax.axis_index(DP)
    data_ranks = lax.axis_size(DP)
    own_flow = flows[data_rank, 0]
    left_flow = flows[(data_rank + data_ranks - 1) % data_ranks, 0]
    live_count = TOK_DEV + own_flow - left_flow
    head_rows = rollout[:MOVE]
    tail_rows = lax.dynamic_slice_in_dim(rollout, live_count - MOVE, MOVE, 0)
    border = extended(jnp.concatenate([head_rows, tail_rows], axis=0), ((DP, 0),), MOVE)
    balanced = settle(rollout, border[:MOVE], border[3 * MOVE :], live_count, left_flow)
    experts_here = lax.axis_size("fsdp")
    outgoing = dispatch_rows(balanced, route_ids, experts_here)
    slot_rows = lax.all_to_all(outgoing, "fsdp", split_axis=0, concat_axis=0, tiled=True)
    sources = slot_rows.shape[0]
    slot_count = slot_rows.shape[1]
    computed = expert_apply(
        slot_rows.reshape(sources * slot_count, D), w_gate[0], w_up[0], w_down[0]
    )
    returned = lax.all_to_all(
        computed.reshape(sources, slot_count, D), "fsdp", split_axis=0, concat_axis=0, tiled=True
    )
    layer_out, router_term = combine(
        balanced, route_ids, route_logits, grad_out, returned, experts_here
    )
    router_grad = router_sum(router_term)
    return (layer_out, router_grad)


def solution(mesh):
    fine = Mesh(mesh.devices.reshape(2, 12, 32), ("yl", "z", "fsdp"))
    rows = P(("yl", "z", "fsdp"), None)
    return jax.shard_map(
        shards,
        mesh=fine,
        in_specs=(
            rows,
            P(None, "fsdp"),
            rows,
            rows,
            rows,
            P("fsdp", None, None),
            P("fsdp", None, None),
            P("fsdp", None, None),
        ),
        out_specs=(rows, P("fsdp", None)),
        check_vma=False,
    )
```

```python
import jax
import jax.numpy as jnp
from jax import lax
from jax.experimental import pallas as pl
from jax.experimental.pallas import tpu as pltpu
from jax.sharding import Mesh
from jax.sharding import PartitionSpec as P

D = 2048
HALF = D // 2
QUARTER = D // 4
FF = 768
EXPERTS = 128
WIN = 32
TOPK = 8
TOK_DEV = 128
SRC_DEV = 192
MOVE = 32
CAP = 12
PAIR = 2 * CAP
ROWS = WIN * PAIR
SLOTS = WIN * CAP
BLOCK = 8 * PAIR
DP = ("yl", "z")
FF_CHUNK = 256
bf16, f32, i32 = jnp.bfloat16, jnp.float32, jnp.int32
VMEM = pl.BlockSpec(memory_space=pltpu.VMEM)
SMEM = pl.BlockSpec(memory_space=pltpu.SMEM)
ANY = pl.BlockSpec(memory_space=pl.ANY)


def iota(shape, dim):
    return lax.broadcasted_iota(i32, shape, dim)


def mm(a, b):
    return jnp.dot(a, b, preferred_element_type=f32)


def whole_div(v, by):
    return jnp.floor((v.astype(f32) + 0.5) * (1.0 / by)).astype(i32)


def split2(v):
    high = v.astype(bf16)
    return high, (v - high.astype(f32)).astype(bf16)


def call(kernel, outs, in_specs, flops, scratch=(), limit=24 << 20):
    many = isinstance(outs, list)
    nbytes = sum(o.size * o.dtype.itemsize for o in (outs if many else [outs]))
    return pl.pallas_call(
        kernel,
        out_shape=outs,
        in_specs=in_specs,
        out_specs=[VMEM] * len(outs) if many else VMEM,
        scratch_shapes=list(scratch),
        cost_estimate=pl.CostEstimate(
            flops=flops, bytes_accessed=2 * nbytes, transcendentals=0
        ),
        compiler_params=pltpu.CompilerParams(vmem_limit_bytes=limit),
    )


def live_of(rank_ref, flows_ref):
    rank = rank_ref[0]
    own = flows_ref[0, rank]
    left = flows_ref[0, jnp.where(rank == 0, 23, rank - 1)]
    return left, TOK_DEV + own - left


def border_kernel(rank_ref, flows_ref, rollout_ref, head_ref, tail_ref):
    _, live = live_of(rank_ref, flows_ref)
    at = iota((MOVE, SRC_DEV), 0) + (live - MOVE)
    pick = (iota((MOVE, SRC_DEV), 1) == at).astype(bf16)
    head_ref[...] = rollout_ref[:MOVE, :]
    tail_ref[...] = mm(pick, rollout_ref[...]).astype(bf16)


def route_kernel(ids_ref, logits_ref, place_ref, weight_ref, high_ref, low_ref):
    logits = logits_ref[...]
    raised = jnp.exp(logits - jnp.max(logits, axis=0, keepdims=True))
    share = raised / jnp.sum(raised, axis=0, keepdims=True)
    expert = iota((EXPERTS, TOK_DEV), 0)
    weight = jnp.zeros((EXPERTS, TOK_DEV), f32)
    named = jnp.zeros((EXPERTS, TOK_DEV), f32)
    for k in range(TOPK):
        hit = ids_ref[k : k + 1, :] == expert
        weight = jnp.where(hit, share[k : k + 1, :], weight)
        named = jnp.where(hit, 1.0, named)
    weight_ref[...] = weight
    upto = (iota((TOK_DEV, TOK_DEV), 0) <= iota((TOK_DEV, TOK_DEV), 1)).astype(bf16)
    count = mm(named[:WIN].astype(bf16), upto)
    code = jnp.where(named[:WIN] > 0.0, count, 0.0).astype(bf16)
    row, of = iota((ROWS, WIN), 0), iota((ROWS, WIN), 1)
    spread = ((row >= of * PAIR) & (row < of * PAIR + PAIR)).astype(bf16)
    high, low = split2(weight[:WIN])
    rows = iota((ROWS, TOK_DEV), 0)
    within = rows - PAIR * whole_div(rows, PAIR)
    second = within >= CAP
    slot = (within - jnp.where(second, CAP, 0) + 1).astype(f32)
    here = mm(spread, code) == slot
    for half in range(2):
        mine = here & (second == (half == 1))
        cols = slice(half * TOK_DEV, (half + 1) * TOK_DEV)
        place_ref[:, cols] = mine.astype(bf16)
        for part, out in ((high, high_ref), (low, low_ref)):
            out[cols, :] = jnp.where(mine, mm(spread, part), 0.0).T.astype(bf16)


def dispatch_kernel(
    rank_ref, flows_ref, left_ref, right_ref, rollout_ref, place_ref, out_ref, bal_ref
):
    left, live = live_of(rank_ref, flows_ref)
    span = SRC_DEV + 2 * MOVE
    at = iota((TOK_DEV, span), 0) + (MOVE - left)
    at = jnp.where(at < MOVE + live, at, at + (SRC_DEV - live))
    settle = (iota((TOK_DEV, span), 1) == at).astype(bf16)
    for half in range(2):
        cols = slice(half * HALF, (half + 1) * HALF)
        rows = jnp.concatenate(
            [left_ref[:, cols], rollout_ref[:, cols], right_ref[:, cols]], axis=0
        )
        bal_ref[half * TOK_DEV : (half + 1) * TOK_DEV, :] = mm(settle, rows).astype(bf16)
    out_ref[...] = mm(place_ref[...], bal_ref[...]).astype(bf16)


def block_source(shape, dim):
    row = iota(shape, dim)
    half = (row >= 8 * CAP).astype(i32)
    rest = row - half * (8 * CAP)
    source = whole_div(rest, CAP)
    return PAIR * source + CAP * half + (rest - CAP * source)


def ffn_kernel(
    rows_ref, gate_hbm, up_hbm, down_hbm, out_ref, gate, up, down, x, hidden, sems
):
    parts = FF // FF_CHUNK
    copies = []
    for f in range(parts):
        cols = pl.ds(f * FF_CHUNK, FF_CHUNK)
        copies.append(
            (
                pltpu.make_async_copy(gate_hbm.at[0, :, cols], gate.at[f], sems.at[2 * f]),
                pltpu.make_async_copy(up_hbm.at[0, :, cols], up.at[f], sems.at[2 * f + 1]),
            )
        )
        copies[f][0].start()
        copies[f][1].start()
    down_copy = pltpu.make_async_copy(down_hbm.at[0], down, sems.at[2 * parts])
    down_copy.start()
    ordered = (iota((BLOCK, BLOCK), 1) == block_source((BLOCK, BLOCK), 0)).astype(bf16)
    back = (iota((BLOCK, BLOCK), 0) == block_source((BLOCK, BLOCK), 1)).astype(bf16)
    part_rows = BLOCK // 2
    for b in range(ROWS // BLOCK):
        y = mm(ordered, rows_ref[b * BLOCK : (b + 1) * BLOCK, :]).astype(bf16)
        x[b * part_rows : (b + 1) * part_rows, :HALF] = y[:part_rows]
        x[b * part_rows : (b + 1) * part_rows, HALF:] = y[part_rows:]
    for f in range(parts):
        copies[f][0].wait()
        g = mm(x[...], gate[f])
        copies[f][1].wait()
        u = mm(x[...], up[f])
        act = g / (1.0 + jnp.exp(-g)) * u
        hidden[:, f * FF_CHUNK : (f + 1) * FF_CHUNK] = act.astype(bf16)
    down_copy.wait()
    for half in range(2):
        cols = slice(half * HALF, (half + 1) * HALF)
        x[:, cols] = mm(hidden[...], down[:, cols]).astype(bf16)
    for b in range(ROWS // BLOCK):
        mine = slice(b * part_rows, (b + 1) * part_rows)
        y = jnp.concatenate([x[mine, :HALF], x[mine, HALF:]], axis=0)
        out_ref[b * BLOCK : (b + 1) * BLOCK, :] = mm(back, y).astype(bf16)


def terms_kernel(rows_ref, grad_ref, bal_ref, place_ref, weight_ref, out_ref):
    cotangent = jnp.concatenate([grad_ref[:, :HALF], grad_ref[:, HALF:]], axis=0)
    scores = lax.dot_general(
        rows_ref[...], cotangent, (((1,), (1,)), ((), ())), preferred_element_type=f32
    )
    high, low = split2(scores * place_ref[...].astype(f32))
    of, row = iota((WIN, ROWS), 0), iota((WIN, ROWS), 1)
    gather = ((row >= of * PAIR) & (row < of * PAIR + PAIR)).astype(bf16)
    both = mm(gather, high) + mm(gather, low)
    score = both[:, :TOK_DEV] + both[:, TOK_DEV:]
    weight = weight_ref[...]
    total = jnp.sum(weight[:WIN] * score, axis=0, keepdims=True)
    grad = jnp.concatenate(
        [weight[:WIN] * (score - total), weight[WIN:] * (0.0 - total)], axis=0
    )
    high, low = split2(grad)
    line = iota((2 * EXPERTS, EXPERTS), 0)
    order = (iota((2 * EXPERTS, EXPERTS), 1) == (line >> 3) * 4 + (line & 3)).astype(bf16)
    factor = jnp.concatenate(
        [mm(order, high).astype(bf16), mm(order, low).astype(bf16)], axis=1
    )
    first = (iota((2 * EXPERTS, QUARTER), 0) & 4) == 0
    for half in range(2):
        tokens = bal_ref[half * TOK_DEV : (half + 1) * TOK_DEV, :]
        term = mm(factor, jnp.concatenate([tokens, tokens], axis=0))
        out_ref[half * 2 * EXPERTS : (half + 1) * 2 * EXPERTS, :] = jnp.where(
            first, term[:, :QUARTER], term[:, QUARTER:]
        ).astype(bf16)


def output_kernel(rows_ref, high_ref, low_ref, out_ref):
    rows = rows_ref[...]
    both = mm(high_ref[...], rows) + mm(low_ref[...], rows)
    out_ref[:, :HALF] = both[:TOK_DEV].astype(bf16)
    out_ref[:, HALF:] = both[TOK_DEV:].astype(bf16)


def part_kernel(terms_ref, out_ref):
    part = jnp.sum(terms_ref[...].astype(f32).reshape(64, 8, QUARTER), axis=0)
    two = jnp.concatenate([part, part], axis=0).astype(bf16)
    for i in range(12):
        out_ref[16 * i : 16 * (i + 1), :] = two


def last_kernel(parts_ref, out_ref):
    parts = jnp.sum(parts_ref[...].astype(f32).reshape(2, 12, 8, QUARTER), axis=1)
    for half in range(2):
        for quarter in range(2):
            at = half * HALF + quarter * QUARTER
            out_ref[:, at : at + QUARTER] = parts[half, 4 * quarter : 4 * quarter + 4]


def shape(dims, dtype):
    return jax.ShapeDtypeStruct(dims, dtype)


def exchange(blocks, axes, peers):
    rows, cols = blocks.shape
    apart = blocks.reshape(peers, rows // peers, cols)
    return lax.all_to_all(apart, axes, split_axis=0, concat_axis=0, tiled=True).reshape(rows, cols)


def borders(rank, flows, rollout):
    return call(
        border_kernel, [shape((MOVE, D), bf16)] * 2, [SMEM, SMEM, VMEM], 25_000_000
    )(rank, flows, rollout)


def routes(ids, logits):
    return call(
        route_kernel,
        [
            shape((ROWS, 2 * TOK_DEV), bf16),
            shape((EXPERTS, TOK_DEV), f32),
            shape((2 * TOK_DEV, ROWS), bf16),
            shape((2 * TOK_DEV, ROWS), bf16),
        ],
        [VMEM] * 2,
        500_000_000,
    )(ids, logits)


def dispatch(rank, flows, left, right, rollout, place):
    return call(
        dispatch_kernel,
        [shape((ROWS, HALF), bf16), shape((2 * TOK_DEV, HALF), bf16)],
        [SMEM, SMEM] + [VMEM] * 4,
        550_000_000,
    )(rank, flows, left, right, rollout, place)


def ffn(rows, w_gate, w_up, w_down):
    parts = FF // FF_CHUNK
    return call(
        ffn_kernel,
        shape((ROWS, HALF), bf16),
        [VMEM, ANY, ANY, ANY],
        3_700_000_000,
        [
            pltpu.VMEM((parts, D, FF_CHUNK), bf16),
            pltpu.VMEM((parts, D, FF_CHUNK), bf16),
            pltpu.VMEM((FF, D), bf16),
            pltpu.VMEM((SLOTS, D), bf16),
            pltpu.VMEM((SLOTS, FF), bf16),
            pltpu.SemaphoreType.DMA((2 * parts + 1,)),
        ],
        limit=40 << 20,
    )(rows, w_gate, w_up, w_down)


def router_terms(rows, grad_out, balanced, place, weight):
    return call(terms_kernel, shape((4 * EXPERTS, QUARTER), bf16), [VMEM] * 5, 700_000_000)(
        rows, grad_out, balanced, place, weight
    )


def layer_output(rows, high, low):
    return call(output_kernel, shape((TOK_DEV, D), bf16), [VMEM] * 3, 4_000_000_000)(
        rows, high, low
    )


def partial_sum(terms):
    return call(part_kernel, shape((192, QUARTER), bf16), [VMEM], 1_000_000)(terms)


def last_sum(parts):
    return call(last_kernel, shape((4, D), f32), [VMEM], 1_000_000)(parts)


def shards(rollout, flows, route_ids, route_logits, grad_out, w_gate, w_up, w_down):
    ranks = lax.axis_size(DP)
    rank = lax.axis_index(DP).reshape(1)
    flows = flows.T
    head, tail = borders(rank, flows, rollout)
    left = lax.ppermute(tail, DP, [(i, (i + 1) % ranks) for i in range(ranks)])
    right = lax.ppermute(head, DP, [((i + 1) % ranks, i) for i in range(ranks)])
    place, weight, high, low = routes(route_ids.T, route_logits.T)
    outgoing, balanced = dispatch(rank, flows, left, right, rollout, place)
    rows = exchange(outgoing, "fsdp", WIN)
    computed = ffn(rows, w_gate, w_up, w_down)
    returned = exchange(computed, "fsdp", WIN)
    terms = exchange(router_terms(returned, grad_out, balanced, place, weight), ("yl", "fsdp"), 64)
    layer_out = layer_output(returned, high, low)
    parts = exchange(partial_sum(terms), DP, 24)
    return (layer_out, last_sum(parts))


def solution(mesh):
    fine = Mesh(mesh.devices.reshape(2, 12, 32), ("yl", "z", "fsdp"))
    rows = P(("yl", "z", "fsdp"), None)
    expert = P("fsdp", None, None)
    return jax.shard_map(
        shards,
        mesh=fine,
        in_specs=(rows, P(None, "fsdp"), rows, rows, rows, expert, expert, expert),
        out_specs=(rows, P("fsdp", None)),
        check_vma=False,
    )
```

```python
import jax
import jax.numpy as jnp
from jax import lax
from jax.experimental import pallas as pl
from jax.experimental.pallas import tpu as pltpu
from jax.sharding import Mesh
from jax.sharding import PartitionSpec as P

D = 2048
HALF = D // 2
QUARTER = D // 4
FF = 768
EXPERTS = 128
WIN = 32
TOPK = 8
TOK_DEV = 128
SRC_DEV = 192
MOVE = 32
NEAR = 48
CAP = 12
PAIR = 2 * CAP
ROWS = WIN * PAIR
SLOTS = WIN * CAP
BLOCK = 8 * PAIR
DP = ("yl", "z")
FF_CHUNK = 256
bf16, f32, i32 = jnp.bfloat16, jnp.float32, jnp.int32
VMEM = pl.BlockSpec(memory_space=pltpu.VMEM)
SMEM = pl.BlockSpec(memory_space=pltpu.SMEM)
HBM = pl.BlockSpec(memory_space=pltpu.HBM)


def iota(shape, dim):
    return lax.broadcasted_iota(i32, shape, dim)


def mm(a, b):
    return jnp.dot(a, b, preferred_element_type=f32)


def whole_div(v, by):
    return jnp.floor((v.astype(f32) + 0.5) * (1.0 / by)).astype(i32)


def split2(v):
    high = v.astype(bf16)
    return high, (v - high.astype(f32)).astype(bf16)


def call(kernel, outs, in_specs, flops, scratch=(), limit=24 << 20):
    many = isinstance(outs, list)
    nbytes = sum(o.size * o.dtype.itemsize for o in (outs if many else [outs]))
    return pl.pallas_call(
        kernel,
        out_shape=outs,
        in_specs=in_specs,
        out_specs=[VMEM] * len(outs) if many else VMEM,
        scratch_shapes=list(scratch),
        cost_estimate=pl.CostEstimate(
            flops=flops, bytes_accessed=2 * nbytes, transcendentals=0
        ),
        compiler_params=pltpu.CompilerParams(vmem_limit_bytes=limit),
    )


def live_of(rank_ref, flows_ref):
    rank = rank_ref[0]
    own = flows_ref[0, rank]
    left = flows_ref[0, jnp.where(rank == 0, 23, rank - 1)]
    return left, TOK_DEV + own - left


def border_kernel(rank_ref, flows_hbm, rollout_hbm, head_ref, tail_ref, flows, near, sems):
    head_copy = pltpu.make_async_copy(rollout_hbm.at[pl.ds(0, MOVE)], head_ref, sems.at[0])
    flow_copy = pltpu.make_async_copy(flows_hbm, flows, sems.at[1])
    flow_copy.start()
    head_copy.start()
    flow_copy.wait()
    _, live = live_of(rank_ref, flows)
    begin = pl.multiple_of(jnp.minimum((live - MOVE) >> 4, (SRC_DEV - NEAR) >> 4) * 16, 16)
    near_copy = pltpu.make_async_copy(rollout_hbm.at[pl.ds(begin, NEAR)], near, sems.at[2])
    near_copy.start()
    at = iota((MOVE, NEAR), 0) + (live - MOVE - begin)
    pick = (iota((MOVE, NEAR), 1) == at).astype(bf16)
    near_copy.wait()
    tail_ref[...] = mm(pick, near[...]).astype(bf16)
    head_copy.wait()


def route_kernel(ids_ref, logits_ref, place_ref, weight_ref, high_ref, low_ref):
    logits = logits_ref[...]
    raised = jnp.exp(logits - jnp.max(logits, axis=0, keepdims=True))
    share = raised / jnp.sum(raised, axis=0, keepdims=True)
    expert = iota((EXPERTS, TOK_DEV), 0)
    weight = jnp.zeros((EXPERTS, TOK_DEV), f32)
    named = jnp.zeros((EXPERTS, TOK_DEV), f32)
    for k in range(TOPK):
        hit = ids_ref[k : k + 1, :] == expert
        weight = jnp.where(hit, share[k : k + 1, :], weight)
        named = jnp.where(hit, 1.0, named)
    weight_ref[...] = weight
    upto = (iota((TOK_DEV, TOK_DEV), 0) <= iota((TOK_DEV, TOK_DEV), 1)).astype(bf16)
    count = mm(named[:WIN].astype(bf16), upto)
    code = jnp.where(named[:WIN] > 0.0, count, 0.0).astype(bf16)
    row, of = iota((ROWS, WIN), 0), iota((ROWS, WIN), 1)
    spread = ((row >= of * PAIR) & (row < of * PAIR + PAIR)).astype(bf16)
    high, low = split2(weight[:WIN])
    rows = iota((ROWS, TOK_DEV), 0)
    within = rows - PAIR * whole_div(rows, PAIR)
    second = within >= CAP
    slot = (within - jnp.where(second, CAP, 0) + 1).astype(f32)
    here = mm(spread, code) == slot
    for half in range(2):
        mine = here & (second == (half == 1))
        cols = slice(half * TOK_DEV, (half + 1) * TOK_DEV)
        place_ref[:, cols] = mine.astype(bf16)
        for part, out in ((high, high_ref), (low, low_ref)):
            out[cols, :] = jnp.where(mine, mm(spread, part), 0.0).T.astype(bf16)


def dispatch_kernel(
    rank_ref, flows_ref, left_ref, right_ref, rollout_ref, place_ref, out_ref, bal_ref
):
    left, live = live_of(rank_ref, flows_ref)
    span = SRC_DEV + 2 * MOVE
    at = iota((TOK_DEV, span), 0) + (MOVE - left)
    at = jnp.where(at < MOVE + live, at, at + (SRC_DEV - live))
    settle = (iota((TOK_DEV, span), 1) == at).astype(bf16)
    for half in range(2):
        cols = slice(half * HALF, (half + 1) * HALF)
        rows = jnp.concatenate(
            [left_ref[:, cols], rollout_ref[:, cols], right_ref[:, cols]], axis=0
        )
        bal_ref[half * TOK_DEV : (half + 1) * TOK_DEV, :] = mm(settle, rows).astype(bf16)
    out_ref[...] = mm(place_ref[...], bal_ref[...]).astype(bf16)


def block_source(shape, dim):
    row = iota(shape, dim)
    half = (row >= 8 * CAP).astype(i32)
    rest = row - half * (8 * CAP)
    source = whole_div(rest, CAP)
    return PAIR * source + CAP * half + (rest - CAP * source)


def ffn_kernel(rows_ref, gate_ref, up_ref, down_hbm, out_ref, down, x, hidden, sem):
    down_copy = pltpu.make_async_copy(down_hbm.at[0], down, sem)
    down_copy.start()
    ordered = (iota((BLOCK, BLOCK), 1) == block_source((BLOCK, BLOCK), 0)).astype(bf16)
    back = (iota((BLOCK, BLOCK), 0) == block_source((BLOCK, BLOCK), 1)).astype(bf16)
    part_rows = BLOCK // 2
    for b in range(ROWS // BLOCK):
        y = mm(ordered, rows_ref[b * BLOCK : (b + 1) * BLOCK, :]).astype(bf16)
        x[b * part_rows : (b + 1) * part_rows, :HALF] = y[:part_rows]
        x[b * part_rows : (b + 1) * part_rows, HALF:] = y[part_rows:]
    for f in range(FF // FF_CHUNK):
        cols = slice(f * FF_CHUNK, (f + 1) * FF_CHUNK)
        g = mm(x[...], gate_ref[0, :, cols])
        u = mm(x[...], up_ref[0, :, cols])
        hidden[:, cols] = (g / (1.0 + jnp.exp(-g)) * u).astype(bf16)
    down_copy.wait()
    for half in range(2):
        cols = slice(half * HALF, (half + 1) * HALF)
        x[:, cols] = mm(hidden[...], down[:, cols]).astype(bf16)
    for b in range(ROWS // BLOCK):
        mine = slice(b * part_rows, (b + 1) * part_rows)
        y = jnp.concatenate([x[mine, :HALF], x[mine, HALF:]], axis=0)
        out_ref[b * BLOCK : (b + 1) * BLOCK, :] = mm(back, y).astype(bf16)


def terms_kernel(rows_ref, grad_ref, bal_ref, place_ref, weight_ref, out_ref):
    cotangent = jnp.concatenate([grad_ref[:, :HALF], grad_ref[:, HALF:]], axis=0)
    scores = lax.dot_general(
        rows_ref[...], cotangent, (((1,), (1,)), ((), ())), preferred_element_type=f32
    )
    high, low = split2(scores * place_ref[...].astype(f32))
    of, row = iota((WIN, ROWS), 0), iota((WIN, ROWS), 1)
    gather = ((row >= of * PAIR) & (row < of * PAIR + PAIR)).astype(bf16)
    both = mm(gather, high) + mm(gather, low)
    score = both[:, :TOK_DEV] + both[:, TOK_DEV:]
    weight = weight_ref[...]
    total = jnp.sum(weight[:WIN] * score, axis=0, keepdims=True)
    grad = jnp.concatenate(
        [weight[:WIN] * (score - total), weight[WIN:] * (0.0 - total)], axis=0
    )
    high, low = split2(grad)
    line = iota((2 * EXPERTS, EXPERTS), 0)
    order = (iota((2 * EXPERTS, EXPERTS), 1) == (line >> 3) * 4 + (line & 3)).astype(bf16)
    factor = jnp.concatenate(
        [mm(order, high).astype(bf16), mm(order, low).astype(bf16)], axis=1
    )
    first = (iota((2 * EXPERTS, QUARTER), 0) & 4) == 0
    for half in range(2):
        tokens = bal_ref[half * TOK_DEV : (half + 1) * TOK_DEV, :]
        term = mm(factor, jnp.concatenate([tokens, tokens], axis=0))
        out_ref[half * 2 * EXPERTS : (half + 1) * 2 * EXPERTS, :] = jnp.where(
            first, term[:, :QUARTER], term[:, QUARTER:]
        ).astype(bf16)


def output_kernel(rows_ref, high_ref, low_ref, out_ref):
    rows = rows_ref[...]
    both = mm(high_ref[...], rows) + mm(low_ref[...], rows)
    out_ref[:, :HALF] = both[:TOK_DEV].astype(bf16)
    out_ref[:, HALF:] = both[TOK_DEV:].astype(bf16)


def part_kernel(terms_ref, out_ref):
    part = jnp.sum(terms_ref[...].astype(f32).reshape(64, 8, QUARTER), axis=0)
    two = jnp.concatenate([part, part], axis=0).astype(bf16)
    for i in range(12):
        out_ref[16 * i : 16 * (i + 1), :] = two


def last_kernel(parts_ref, out_ref):
    parts = jnp.sum(parts_ref[...].astype(f32).reshape(2, 12, 8, QUARTER), axis=1)
    for half in range(2):
        for quarter in range(2):
            at = half * HALF + quarter * QUARTER
            out_ref[:, at : at + QUARTER] = parts[half, 4 * quarter : 4 * quarter + 4]


def in_hbm(array):
    return pltpu.with_memory_space_constraint(array, pltpu.HBM)


def shape(dims, dtype):
    return jax.ShapeDtypeStruct(dims, dtype)


def exchange(blocks, axes, peers):
    rows, cols = blocks.shape
    apart = blocks.reshape(peers, rows // peers, cols)
    return lax.all_to_all(apart, axes, split_axis=0, concat_axis=0, tiled=True).reshape(rows, cols)


def borders(rank, flows, rollout):
    return call(
        border_kernel,
        [shape((MOVE, D), bf16)] * 2,
        [SMEM, HBM, HBM],
        25_000_000,
        [
            pltpu.SMEM((1, 24), i32),
            pltpu.VMEM((NEAR, D), bf16),
            pltpu.SemaphoreType.DMA((3,)),
        ],
    )(rank, in_hbm(flows), in_hbm(rollout))


def routes(ids, logits):
    return call(
        route_kernel,
        [
            shape((ROWS, 2 * TOK_DEV), bf16),
            shape((EXPERTS, TOK_DEV), f32),
            shape((2 * TOK_DEV, ROWS), bf16),
            shape((2 * TOK_DEV, ROWS), bf16),
        ],
        [VMEM] * 2,
        500_000_000,
    )(ids, logits)


def dispatch(rank, flows, left, right, rollout, place):
    return call(
        dispatch_kernel,
        [shape((ROWS, HALF), bf16), shape((2 * TOK_DEV, HALF), bf16)],
        [SMEM, SMEM] + [VMEM] * 4,
        550_000_000,
    )(rank, flows, left, right, rollout, place)


def ffn(rows, w_gate, w_up, w_down):
    return call(
        ffn_kernel,
        shape((ROWS, HALF), bf16),
        [VMEM, VMEM, VMEM, HBM],
        3_700_000_000,
        [
            pltpu.VMEM((FF, D), bf16),
            pltpu.VMEM((SLOTS, D), bf16),
            pltpu.VMEM((SLOTS, FF), bf16),
            pltpu.SemaphoreType.DMA,
        ],
    )(rows, w_gate, w_up, in_hbm(w_down))


def router_terms(rows, grad_out, balanced, place, weight):
    return call(terms_kernel, shape((4 * EXPERTS, QUARTER), bf16), [VMEM] * 5, 700_000_000)(
        rows, grad_out, balanced, place, weight
    )


def layer_output(rows, high, low):
    return call(output_kernel, shape((TOK_DEV, D), bf16), [VMEM] * 3, 4_000_000_000)(
        rows, high, low
    )


def partial_sum(terms):
    return call(part_kernel, shape((192, QUARTER), bf16), [VMEM], 1_000_000)(terms)


def last_sum(parts):
    return call(last_kernel, shape((4, D), f32), [VMEM], 1_000_000)(parts)


def shards(rollout, flows, route_ids, route_logits, grad_out, w_gate, w_up, w_down):
    ranks = lax.axis_size(DP)
    rank = lax.axis_index(DP).reshape(1)
    flows = flows.T
    head, tail = borders(rank, flows, rollout)
    left = lax.ppermute(tail, DP, [(i, (i + 1) % ranks) for i in range(ranks)])
    right = lax.ppermute(head, DP, [((i + 1) % ranks, i) for i in range(ranks)])
    place, weight, high, low = routes(route_ids.T, route_logits.T)
    outgoing, balanced = dispatch(rank, flows, left, right, rollout, place)
    rows = exchange(outgoing, "fsdp", WIN)
    computed = ffn(rows, w_gate, w_up, w_down)
    returned = exchange(computed, "fsdp", WIN)
    terms = exchange(router_terms(returned, grad_out, balanced, place, weight), ("yl", "fsdp"), 64)
    layer_out = layer_output(returned, high, low)
    parts = exchange(partial_sum(terms), DP, 24)
    return (layer_out, last_sum(parts))


def solution(mesh):
    fine = Mesh(mesh.devices.reshape(2, 12, 32), ("yl", "z", "fsdp"))
    rows = P(("yl", "z", "fsdp"), None)
    expert = P("fsdp", None, None)
    return jax.shard_map(
        shards,
        mesh=fine,
        in_specs=(rows, P(None, "fsdp"), rows, rows, rows, expert, expert, expert),
        out_specs=(rows, P("fsdp", None)),
        check_vma=False,
    )
```

```python
import jax
import jax.numpy as jnp
from jax import lax
from jax.experimental import pallas as pl
from jax.experimental.pallas import tpu as pltpu
from jax.sharding import Mesh
from jax.sharding import PartitionSpec as P

D = 2048
HALF = D // 2
QUARTER = D // 4
FF = 768
EXPERTS = 128
WIN = 32
TOPK = 8
TOK_DEV = 128
SRC_DEV = 192
MOVE = 32
NEAR = 48
CAP = 12
WHOLE = 8
ROWS = WIN * WHOLE
WIDTH = D + HALF
SLOTS = WIN * CAP
BLOCK = 128
DP = ("yl", "z")
FF_CHUNK = 256
bf16, f32, i32 = jnp.bfloat16, jnp.float32, jnp.int32
VMEM = pl.BlockSpec(memory_space=pltpu.VMEM)
SMEM = pl.BlockSpec(memory_space=pltpu.SMEM)
HBM = pl.BlockSpec(memory_space=pltpu.HBM)


def iota(shape, dim):
    return lax.broadcasted_iota(i32, shape, dim)


def mm(a, b):
    return jnp.dot(a, b, preferred_element_type=f32)


def split2(v):
    high = v.astype(bf16)
    return high, (v - high.astype(f32)).astype(bf16)


def call(kernel, outs, in_specs, flops, scratch=(), limit=24 << 20):
    many = isinstance(outs, list)
    nbytes = sum(o.size * o.dtype.itemsize for o in (outs if many else [outs]))
    return pl.pallas_call(
        kernel,
        out_shape=outs,
        in_specs=in_specs,
        out_specs=[VMEM] * len(outs) if many else VMEM,
        scratch_shapes=list(scratch),
        cost_estimate=pl.CostEstimate(
            flops=flops, bytes_accessed=2 * nbytes, transcendentals=0
        ),
        compiler_params=pltpu.CompilerParams(vmem_limit_bytes=limit),
    )


def live_of(rank_ref, flows_ref):
    rank = rank_ref[0]
    own = flows_ref[0, rank]
    left = flows_ref[0, jnp.where(rank == 0, 23, rank - 1)]
    return left, TOK_DEV + own - left


def border_kernel(
    rank_ref,
    flows_hbm,
    rollout_hbm,
    ids_hbm,
    logits_hbm,
    head_ref,
    tail_ref,
    place_ref,
    late_ref,
    weight_ref,
    high_ref,
    low_ref,
    late_high_ref,
    late_low_ref,
    flows,
    near,
    ids,
    logits,
    sems,
):
    flow_copy = pltpu.make_async_copy(flows_hbm, flows, sems.at[0])
    ids_copy = pltpu.make_async_copy(ids_hbm, ids, sems.at[1])
    logits_copy = pltpu.make_async_copy(logits_hbm, logits, sems.at[2])
    head_copy = pltpu.make_async_copy(rollout_hbm.at[pl.ds(0, MOVE)], head_ref, sems.at[3])
    flow_copy.start()
    ids_copy.start()
    logits_copy.start()
    head_copy.start()
    flow_copy.wait()
    _, live = live_of(rank_ref, flows)
    begin = pl.multiple_of(jnp.minimum((live - MOVE) >> 4, (SRC_DEV - NEAR) >> 4) * 16, 16)
    near_copy = pltpu.make_async_copy(rollout_hbm.at[pl.ds(begin, NEAR)], near, sems.at[4])
    near_copy.start()
    ids_copy.wait()
    logits_copy.wait()
    route(
        ids,
        logits[...],
        place_ref,
        late_ref,
        weight_ref,
        (high_ref, low_ref),
        (late_high_ref, late_low_ref),
    )
    at = iota((MOVE, NEAR), 0) + (live - MOVE - begin)
    pick = (iota((MOVE, NEAR), 1) == at).astype(bf16)
    near_copy.wait()
    tail_ref[...] = mm(pick, near[...]).astype(bf16)
    head_copy.wait()


def route(ids, logits, place_ref, late_ref, weight_ref, parts_refs, late_parts_refs):
    raised = jnp.exp(logits - jnp.max(logits, axis=0, keepdims=True))
    share = raised / jnp.sum(raised, axis=0, keepdims=True)
    expert = iota((EXPERTS, TOK_DEV), 0)
    weight = jnp.zeros((EXPERTS, TOK_DEV), f32)
    named = jnp.zeros((EXPERTS, TOK_DEV), f32)
    for k in range(TOPK):
        hit = ids[k : k + 1, :] == expert
        weight = jnp.where(hit, share[k : k + 1, :], weight)
        named = jnp.where(hit, 1.0, named)
    weight_ref[...] = weight
    upto = (iota((TOK_DEV, TOK_DEV), 0) <= iota((TOK_DEV, TOK_DEV), 1)).astype(bf16)
    count = mm(named[:WIN].astype(bf16), upto)
    code = jnp.where(named[:WIN] > 0.0, count, 0.0).astype(bf16)
    spread = ((iota((ROWS, WIN), 0) >> 3) == iota((ROWS, WIN), 1)).astype(bf16)
    row = iota((ROWS, TOK_DEV), 0)
    codes = mm(spread, code).astype(i32)
    whole = codes == (row & 7) + 1
    late = codes == (row & 3) + (WHOLE + 1)
    second = (row & 4) == 4
    place_ref[...] = whole.astype(bf16)
    for half in range(2):
        cols = slice(half * TOK_DEV, (half + 1) * TOK_DEV)
        late_ref[:, cols] = (late & (second == (half == 1))).astype(bf16)
    for part, out, late_out in zip(split2(weight[:WIN]), parts_refs, late_parts_refs):
        spreads = mm(spread, part)
        out[...] = jnp.where(whole, spreads, 0.0).T.astype(bf16)
        for half in range(2):
            mine = late & (second == (half == 1))
            late_out[half * TOK_DEV : (half + 1) * TOK_DEV, :] = (
                jnp.where(mine, spreads, 0.0).T.astype(bf16)
            )


def halves(wide):
    return jnp.concatenate([wide[:, :HALF], wide[:, HALF:]], axis=0)


def dispatch_kernel(
    rank_ref,
    flows_ref,
    left_ref,
    right_ref,
    rollout_ref,
    place_ref,
    late_ref,
    out_ref,
    bal_ref,
):
    left, live = live_of(rank_ref, flows_ref)
    span = SRC_DEV + 2 * MOVE
    at = iota((TOK_DEV, span), 0) + (MOVE - left)
    at = jnp.where(at < MOVE + live, at, at + (SRC_DEV - live))
    settle = (iota((TOK_DEV, span), 1) == at).astype(bf16)
    rows = jnp.concatenate([left_ref[...], rollout_ref[...], right_ref[...]], axis=0)
    balanced = mm(settle, rows).astype(bf16)
    bal_ref[...] = balanced
    out_ref[:, :D] = mm(place_ref[...], balanced).astype(bf16)
    out_ref[:, D:] = mm(late_ref[...], halves(balanced)).astype(bf16)


def block_source(dim):
    row = iota((BLOCK, BLOCK), dim)
    return ((row >> 2) & 15) * 8 + (row >> 6) * 4 + (row & 3)


def ffn_kernel(rows_ref, gate_ref, up_ref, down_hbm, out_ref, down, x, hidden, sem):
    down_copy = pltpu.make_async_copy(down_hbm.at[0], down, sem)
    down_copy.start()
    ordered = (iota((BLOCK, BLOCK), 1) == block_source(0)).astype(bf16)
    back = (iota((BLOCK, BLOCK), 0) == block_source(1)).astype(bf16)
    part_rows = BLOCK // 2
    x[:ROWS, :] = rows_ref[:, :D]
    for b in range(ROWS // BLOCK):
        y = mm(ordered, rows_ref[b * BLOCK : (b + 1) * BLOCK, D:]).astype(bf16)
        mine = slice(ROWS + b * part_rows, ROWS + (b + 1) * part_rows)
        x[mine, :HALF] = y[:part_rows]
        x[mine, HALF:] = y[part_rows:]
    for f in range(FF // FF_CHUNK):
        cols = slice(f * FF_CHUNK, (f + 1) * FF_CHUNK)
        g = mm(x[...], gate_ref[0, :, cols])
        u = mm(x[...], up_ref[0, :, cols])
        hidden[:, cols] = (g / (1.0 + jnp.exp(-g)) * u).astype(bf16)
    down_copy.wait()
    late = []
    for half in range(2):
        cols = slice(half * HALF, (half + 1) * HALF)
        y = mm(hidden[...], down[:, cols]).astype(bf16)
        out_ref[:, cols] = y[:ROWS]
        late.append(y[ROWS:])
    for b in range(ROWS // BLOCK):
        mine = slice(b * part_rows, (b + 1) * part_rows)
        y = jnp.concatenate([late[0][mine], late[1][mine]], axis=0)
        out_ref[b * BLOCK : (b + 1) * BLOCK, D:] = mm(back, y).astype(bf16)


def against(a, b):
    return lax.dot_general(a, b, (((1,), (1,)), ((), ())), preferred_element_type=f32)


def terms_kernel(rows_ref, grad_ref, bal_ref, place_ref, late_ref, weight_ref, out_ref):
    cotangent = grad_ref[...]
    scores = against(rows_ref[:, :D], cotangent) * place_ref[...].astype(f32)
    late = against(rows_ref[:, D:], halves(cotangent)) * late_ref[...].astype(f32)
    scores = scores + late[:, :TOK_DEV] + late[:, TOK_DEV:]
    score = jnp.sum(scores.reshape(WIN, WHOLE, TOK_DEV), axis=1)
    weight = weight_ref[...]
    total = jnp.sum(weight[:WIN] * score, axis=0, keepdims=True)
    grad = jnp.concatenate(
        [weight[:WIN] * (score - total), weight[WIN:] * (0.0 - total)], axis=0
    )
    high, low = split2(grad)
    line = iota((2 * EXPERTS, EXPERTS), 0)
    order = (iota((2 * EXPERTS, EXPERTS), 1) == (line >> 3) * 4 + (line & 3)).astype(bf16)
    factor = jnp.concatenate(
        [mm(order, high).astype(bf16), mm(order, low).astype(bf16)], axis=1
    )
    first = (iota((2 * EXPERTS, QUARTER), 0) & 4) == 0
    for half in range(2):
        tokens = bal_ref[:, half * HALF : (half + 1) * HALF]
        term = mm(factor, jnp.concatenate([tokens, tokens], axis=0))
        out_ref[half * 2 * EXPERTS : (half + 1) * 2 * EXPERTS, :] = jnp.where(
            first, term[:, :QUARTER], term[:, QUARTER:]
        ).astype(bf16)


def output_kernel(rows_ref, high_ref, low_ref, late_high_ref, late_low_ref, out_ref):
    rows, ends = rows_ref[:, :D], rows_ref[:, D:]
    late = mm(late_high_ref[...], ends) + mm(late_low_ref[...], ends)
    both = mm(high_ref[...], rows) + mm(low_ref[...], rows)
    out_ref[:, :HALF] = (both[:, :HALF] + late[:TOK_DEV]).astype(bf16)
    out_ref[:, HALF:] = (both[:, HALF:] + late[TOK_DEV:]).astype(bf16)


def part_kernel(terms_ref, out_ref):
    part = jnp.sum(terms_ref[...].astype(f32).reshape(64, 8, QUARTER), axis=0)
    two = jnp.concatenate([part, part], axis=0).astype(bf16)
    for i in range(12):
        out_ref[16 * i : 16 * (i + 1), :] = two


def last_kernel(parts_ref, out_ref):
    parts = jnp.sum(parts_ref[...].astype(f32).reshape(2, 12, 8, QUARTER), axis=1)
    for half in range(2):
        for quarter in range(2):
            at = half * HALF + quarter * QUARTER
            out_ref[:, at : at + QUARTER] = parts[half, 4 * quarter : 4 * quarter + 4]


def in_hbm(array):
    return pltpu.with_memory_space_constraint(array, pltpu.HBM)


def shape(dims, dtype):
    return jax.ShapeDtypeStruct(dims, dtype)


def exchange(blocks, axes, peers):
    rows, cols = blocks.shape
    apart = blocks.reshape(peers, rows // peers, cols)
    return lax.all_to_all(apart, axes, split_axis=0, concat_axis=0, tiled=True).reshape(rows, cols)


def borders(rank, flows, rollout, ids, logits):
    return call(
        border_kernel,
        [
            shape((MOVE, D), bf16),
            shape((MOVE, D), bf16),
            shape((ROWS, TOK_DEV), bf16),
            shape((ROWS, 2 * TOK_DEV), bf16),
            shape((EXPERTS, TOK_DEV), f32),
            shape((TOK_DEV, ROWS), bf16),
            shape((TOK_DEV, ROWS), bf16),
            shape((2 * TOK_DEV, ROWS), bf16),
            shape((2 * TOK_DEV, ROWS), bf16),
        ],
        [SMEM] + [HBM] * 4,
        25_000_000,
        [
            pltpu.SMEM((1, 24), i32),
            pltpu.VMEM((NEAR, D), bf16),
            pltpu.VMEM((TOPK, TOK_DEV), i32),
            pltpu.VMEM((TOPK, TOK_DEV), f32),
            pltpu.SemaphoreType.DMA((5,)),
        ],
    )(rank, *[in_hbm(v) for v in (flows, rollout, ids, logits)])


def dispatch(rank, flows, left, right, rollout, place, late):
    return call(
        dispatch_kernel,
        [shape((ROWS, WIDTH), bf16), shape((TOK_DEV, D), bf16)],
        [SMEM, SMEM] + [VMEM] * 5,
        550_000_000,
    )(rank, flows, left, right, rollout, place, late)


def ffn(rows, w_gate, w_up, w_down):
    return call(
        ffn_kernel,
        shape((ROWS, WIDTH), bf16),
        [VMEM, VMEM, VMEM, HBM],
        3_700_000_000,
        [
            pltpu.VMEM((FF, D), bf16),
            pltpu.VMEM((SLOTS, D), bf16),
            pltpu.VMEM((SLOTS, FF), bf16),
            pltpu.SemaphoreType.DMA,
        ],
    )(rows, w_gate, w_up, in_hbm(w_down))


def router_terms(rows, grad_out, balanced, place, late, weight):
    return call(terms_kernel, shape((4 * EXPERTS, QUARTER), bf16), [VMEM] * 6, 700_000_000)(
        rows, grad_out, balanced, place, late, weight
    )


def layer_output(rows, high, low, late_high, late_low):
    return call(output_kernel, shape((TOK_DEV, D), bf16), [VMEM] * 5, 4_000_000_000)(
        rows, high, low, late_high, late_low
    )


def partial_sum(terms):
    return call(part_kernel, shape((192, QUARTER), bf16), [VMEM], 1_000_000)(terms)


def last_sum(parts):
    return call(last_kernel, shape((4, D), f32), [VMEM], 1_000_000)(parts)


def shards(rollout, flows, route_ids, route_logits, grad_out, w_gate, w_up, w_down):
    ranks = lax.axis_size(DP)
    rank = lax.axis_index(DP).reshape(1)
    flows = flows.T
    head, tail, place, late, weight, *shares = borders(
        rank, flows, rollout, route_ids.T, route_logits.T
    )
    left = lax.ppermute(tail, DP, [(i, (i + 1) % ranks) for i in range(ranks)])
    right = lax.ppermute(head, DP, [((i + 1) % ranks, i) for i in range(ranks)])
    outgoing, balanced = dispatch(rank, flows, left, right, rollout, place, late)
    rows = exchange(outgoing, "fsdp", WIN)
    computed = ffn(rows, w_gate, w_up, w_down)
    returned = exchange(computed, "fsdp", WIN)
    terms = router_terms(returned, grad_out, balanced, place, late, weight)
    terms = exchange(terms, ("yl", "fsdp"), 64)
    layer_out = layer_output(returned, *shares)
    parts = exchange(partial_sum(terms), DP, 24)
    return (layer_out, last_sum(parts))


def solution(mesh):
    fine = Mesh(mesh.devices.reshape(2, 12, 32), ("yl", "z", "fsdp"))
    rows = P(("yl", "z", "fsdp"), None)
    expert = P("fsdp", None, None)
    return jax.shard_map(
        shards,
        mesh=fine,
        in_specs=(rows, P(None, "fsdp"), rows, rows, rows, expert, expert, expert),
        out_specs=(rows, P("fsdp", None)),
        check_vma=False,
    )
```

```python
import jax
import jax.numpy as jnp
from jax import lax
from jax.experimental import pallas as pl
from jax.experimental.pallas import tpu as pltpu
from jax.sharding import Mesh
from jax.sharding import PartitionSpec as P

D = 2048
HALF = D // 2
QUARTER = D // 4
FF = 768
EXPERTS = 128
WIN = 32
TOPK = 8
TOK_DEV = 128
SRC_DEV = 192
MOVE = 32
CAP = 12
SPAN = SRC_DEV + 2 * MOVE
WHOLE = 8
ROWS = WIN * WHOLE
WIDTH = D + HALF
SLOTS = WIN * CAP
BLOCK = 128
DP = ("yl", "z")
FF_CHUNK = 256
bf16, f32, i32 = jnp.bfloat16, jnp.float32, jnp.int32
VMEM = pl.BlockSpec(memory_space=pltpu.VMEM)
SMEM = pl.BlockSpec(memory_space=pltpu.SMEM)
HBM = pl.BlockSpec(memory_space=pltpu.HBM)


def iota(shape, dim):
    return lax.broadcasted_iota(i32, shape, dim)


def mm(a, b):
    return jnp.dot(a, b, preferred_element_type=f32)


def split2(v):
    high = v.astype(bf16)
    return high, (v - high.astype(f32)).astype(bf16)


def call(kernel, outs, in_specs, flops, scratch=(), limit=24 << 20):
    many = isinstance(outs, list)
    nbytes = sum(o.size * o.dtype.itemsize for o in (outs if many else [outs]))
    return pl.pallas_call(
        kernel,
        out_shape=outs,
        in_specs=in_specs,
        out_specs=[VMEM] * len(outs) if many else VMEM,
        scratch_shapes=list(scratch),
        cost_estimate=pl.CostEstimate(
            flops=flops, bytes_accessed=2 * nbytes, transcendentals=0
        ),
        compiler_params=pltpu.CompilerParams(vmem_limit_bytes=limit),
    )


def border_kernel(
    rank_ref,
    flows_hbm,
    rollout_hbm,
    ids_hbm,
    logits_hbm,
    head_ref,
    tail_ref,
    held_ref,
    settle_ref,
    place_ref,
    late_ref,
    weight_ref,
    high_ref,
    low_ref,
    late_high_ref,
    late_low_ref,
    flows,
    ids,
    logits,
    sems,
):
    flow_copy = pltpu.make_async_copy(flows_hbm, flows, sems.at[0])
    ids_copy = pltpu.make_async_copy(ids_hbm, ids, sems.at[1])
    logits_copy = pltpu.make_async_copy(logits_hbm, logits, sems.at[2])
    held_copy = pltpu.make_async_copy(rollout_hbm, held_ref, sems.at[3])
    flow_copy.start()
    ids_copy.start()
    logits_copy.start()
    held_copy.start()
    ids_copy.wait()
    logits_copy.wait()
    route(
        ids,
        logits[...],
        place_ref,
        late_ref,
        weight_ref,
        (high_ref, low_ref),
        (late_high_ref, late_low_ref),
    )
    flow_copy.wait()
    rank = rank_ref[0]
    left = flows[0, jnp.where(rank == 0, 23, rank - 1)]
    live = TOK_DEV + flows[0, rank] - left
    at = iota((TOK_DEV, SPAN), 0) + (MOVE - left)
    at = jnp.where(at < MOVE + live, at, at + (SRC_DEV - live))
    settle_ref[...] = (iota((TOK_DEV, SPAN), 1) == at).astype(bf16)
    at = iota((MOVE, SRC_DEV), 0) + (live - MOVE)
    pick = (iota((MOVE, SRC_DEV), 1) == at).astype(bf16)
    held_copy.wait()
    head_ref[...] = held_ref[:MOVE, :]
    tail_ref[...] = mm(pick, held_ref[...]).astype(bf16)


def route(ids, logits, place_ref, late_ref, weight_ref, parts_refs, late_parts_refs):
    raised = jnp.exp(logits - jnp.max(logits, axis=0, keepdims=True))
    share = raised / jnp.sum(raised, axis=0, keepdims=True)
    expert = iota((EXPERTS, TOK_DEV), 0)
    weight = jnp.zeros((EXPERTS, TOK_DEV), f32)
    named = jnp.zeros((EXPERTS, TOK_DEV), f32)
    for k in range(TOPK):
        hit = ids[k : k + 1, :] == expert
        weight = jnp.where(hit, share[k : k + 1, :], weight)
        named = jnp.where(hit, 1.0, named)
    weight_ref[...] = weight
    upto = (iota((TOK_DEV, TOK_DEV), 0) <= iota((TOK_DEV, TOK_DEV), 1)).astype(bf16)
    count = mm(named[:WIN].astype(bf16), upto)
    code = jnp.where(named[:WIN] > 0.0, count, 0.0).astype(bf16)
    spread = ((iota((ROWS, WIN), 0) >> 3) == iota((ROWS, WIN), 1)).astype(bf16)
    row = iota((ROWS, TOK_DEV), 0)
    codes = mm(spread, code).astype(i32)
    whole = codes == (row & 7) + 1
    late = codes == (row & 3) + (WHOLE + 1)
    second = (row & 4) == 4
    place_ref[...] = whole.astype(bf16)
    for half in range(2):
        cols = slice(half * TOK_DEV, (half + 1) * TOK_DEV)
        late_ref[:, cols] = (late & (second == (half == 1))).astype(bf16)
    for part, out, late_out in zip(split2(weight[:WIN]), parts_refs, late_parts_refs):
        spreads = mm(spread, part)
        out[...] = jnp.where(whole, spreads, 0.0).T.astype(bf16)
        for half in range(2):
            mine = late & (second == (half == 1))
            late_out[half * TOK_DEV : (half + 1) * TOK_DEV, :] = (
                jnp.where(mine, spreads, 0.0).T.astype(bf16)
            )


def halves(wide):
    return jnp.concatenate([wide[:, :HALF], wide[:, HALF:]], axis=0)


def dispatch_kernel(
    left_ref, right_ref, held_ref, settle_ref, place_ref, late_ref, out_ref, bal_ref
):
    rows = jnp.concatenate([left_ref[...], held_ref[...], right_ref[...]], axis=0)
    balanced = mm(settle_ref[...], rows).astype(bf16)
    bal_ref[...] = balanced
    out_ref[:, :D] = mm(place_ref[...], balanced).astype(bf16)
    out_ref[:, D:] = mm(late_ref[...], halves(balanced)).astype(bf16)


def block_source(dim):
    row = iota((BLOCK, BLOCK), dim)
    return ((row >> 2) & 15) * 8 + (row >> 6) * 4 + (row & 3)


def ffn_kernel(rows_ref, gate_ref, up_hbm, down_hbm, out_ref, up, down, x, hidden, sems):
    parts = FF // FF_CHUNK
    up_copies = []
    for f in range(parts):
        cols = pl.ds(f * FF_CHUNK, FF_CHUNK)
        up_copies.append(pltpu.make_async_copy(up_hbm.at[0, :, cols], up.at[f], sems.at[f]))
        up_copies[f].start()
    down_copy = pltpu.make_async_copy(down_hbm.at[0], down, sems.at[parts])
    down_copy.start()
    ordered = (iota((BLOCK, BLOCK), 1) == block_source(0)).astype(bf16)
    back = (iota((BLOCK, BLOCK), 0) == block_source(1)).astype(bf16)
    part_rows = BLOCK // 2
    x[:ROWS, :] = rows_ref[:, :D]
    for b in range(ROWS // BLOCK):
        y = mm(ordered, rows_ref[b * BLOCK : (b + 1) * BLOCK, D:]).astype(bf16)
        mine = slice(ROWS + b * part_rows, ROWS + (b + 1) * part_rows)
        x[mine, :HALF] = y[:part_rows]
        x[mine, HALF:] = y[part_rows:]
    gates = [
        mm(x[...], gate_ref[0, :, f * FF_CHUNK : (f + 1) * FF_CHUNK]) for f in range(parts)
    ]
    for f, g in enumerate(gates):
        up_copies[f].wait()
        u = mm(x[...], up[f])
        cols = slice(f * FF_CHUNK, (f + 1) * FF_CHUNK)
        hidden[:, cols] = (g / (1.0 + jnp.exp(-g)) * u).astype(bf16)
    down_copy.wait()
    late = []
    for half in range(2):
        cols = slice(half * HALF, (half + 1) * HALF)
        y = mm(hidden[...], down[:, cols]).astype(bf16)
        out_ref[:, cols] = y[:ROWS]
        late.append(y[ROWS:])
    for b in range(ROWS // BLOCK):
        mine = slice(b * part_rows, (b + 1) * part_rows)
        y = jnp.concatenate([late[0][mine], late[1][mine]], axis=0)
        out_ref[b * BLOCK : (b + 1) * BLOCK, D:] = mm(back, y).astype(bf16)


def against(a, b):
    return lax.dot_general(a, b, (((1,), (1,)), ((), ())), preferred_element_type=f32)


def terms_kernel(rows_ref, grad_ref, bal_ref, place_ref, late_ref, weight_ref, out_ref):
    cotangent = grad_ref[...]
    scores = against(rows_ref[:, :D], cotangent) * place_ref[...].astype(f32)
    late = against(rows_ref[:, D:], halves(cotangent)) * late_ref[...].astype(f32)
    scores = scores + late[:, :TOK_DEV] + late[:, TOK_DEV:]
    score = jnp.sum(scores.reshape(WIN, WHOLE, TOK_DEV), axis=1)
    weight = weight_ref[...]
    total = jnp.sum(weight[:WIN] * score, axis=0, keepdims=True)
    grad = jnp.concatenate(
        [weight[:WIN] * (score - total), weight[WIN:] * (0.0 - total)], axis=0
    )
    high, low = split2(grad)
    line = iota((2 * EXPERTS, EXPERTS), 0)
    order = (iota((2 * EXPERTS, EXPERTS), 1) == (line >> 3) * 4 + (line & 3)).astype(bf16)
    factor = jnp.concatenate(
        [mm(order, high).astype(bf16), mm(order, low).astype(bf16)], axis=1
    )
    first = (iota((2 * EXPERTS, QUARTER), 0) & 4) == 0
    for half in range(2):
        tokens = bal_ref[:, half * HALF : (half + 1) * HALF]
        term = mm(factor, jnp.concatenate([tokens, tokens], axis=0))
        out_ref[half * 2 * EXPERTS : (half + 1) * 2 * EXPERTS, :] = jnp.where(
            first, term[:, :QUARTER], term[:, QUARTER:]
        ).astype(bf16)


def output_kernel(rows_ref, high_ref, low_ref, late_high_ref, late_low_ref, out_ref):
    rows, ends = rows_ref[:, :D], rows_ref[:, D:]
    late = mm(late_high_ref[...], ends) + mm(late_low_ref[...], ends)
    both = mm(high_ref[...], rows) + mm(low_ref[...], rows)
    out_ref[:, :HALF] = (both[:, :HALF] + late[:TOK_DEV]).astype(bf16)
    out_ref[:, HALF:] = (both[:, HALF:] + late[TOK_DEV:]).astype(bf16)


def part_kernel(terms_ref, out_ref):
    part = jnp.sum(terms_ref[...].astype(f32).reshape(64, 8, QUARTER), axis=0)
    two = jnp.concatenate([part, part], axis=0).astype(bf16)
    for i in range(12):
        out_ref[16 * i : 16 * (i + 1), :] = two


def last_kernel(parts_ref, out_ref):
    parts = jnp.sum(parts_ref[...].astype(f32).reshape(2, 12, 8, QUARTER), axis=1)
    for half in range(2):
        for quarter in range(2):
            at = half * HALF + quarter * QUARTER
            out_ref[:, at : at + QUARTER] = parts[half, 4 * quarter : 4 * quarter + 4]


def in_hbm(array):
    return pltpu.with_memory_space_constraint(array, pltpu.HBM)


def shape(dims, dtype):
    return jax.ShapeDtypeStruct(dims, dtype)


def exchange(blocks, axes, peers):
    rows, cols = blocks.shape
    apart = blocks.reshape(peers, rows // peers, cols)
    return lax.all_to_all(apart, axes, split_axis=0, concat_axis=0, tiled=True).reshape(rows, cols)


def borders(rank, flows, rollout, ids, logits):
    return call(
        border_kernel,
        [
            shape((MOVE, D), bf16),
            shape((MOVE, D), bf16),
            shape((SRC_DEV, D), bf16),
            shape((TOK_DEV, SPAN), bf16),
            shape((ROWS, TOK_DEV), bf16),
            shape((ROWS, 2 * TOK_DEV), bf16),
            shape((EXPERTS, TOK_DEV), f32),
            shape((TOK_DEV, ROWS), bf16),
            shape((TOK_DEV, ROWS), bf16),
            shape((2 * TOK_DEV, ROWS), bf16),
            shape((2 * TOK_DEV, ROWS), bf16),
        ],
        [SMEM] + [HBM] * 4,
        25_000_000,
        [
            pltpu.SMEM((1, 24), i32),
            pltpu.VMEM((TOPK, TOK_DEV), i32),
            pltpu.VMEM((TOPK, TOK_DEV), f32),
            pltpu.SemaphoreType.DMA((4,)),
        ],
    )(rank, *[in_hbm(v) for v in (flows, rollout, ids, logits)])


def dispatch(left, right, held, settle, place, late):
    return call(
        dispatch_kernel,
        [shape((ROWS, WIDTH), bf16), shape((TOK_DEV, D), bf16)],
        [VMEM] * 6,
        550_000_000,
    )(left, right, held, settle, place, late)


def ffn(rows, w_gate, w_up, w_down):
    return call(
        ffn_kernel,
        shape((ROWS, WIDTH), bf16),
        [VMEM, VMEM, HBM, HBM],
        3_700_000_000,
        [
            pltpu.VMEM((FF // FF_CHUNK, D, FF_CHUNK), bf16),
            pltpu.VMEM((FF, D), bf16),
            pltpu.VMEM((SLOTS, D), bf16),
            pltpu.VMEM((SLOTS, FF), bf16),
            pltpu.SemaphoreType.DMA((FF // FF_CHUNK + 1,)),
        ],
    )(rows, w_gate, in_hbm(w_up), in_hbm(w_down))


def router_terms(rows, grad_out, balanced, place, late, weight):
    return call(terms_kernel, shape((4 * EXPERTS, QUARTER), bf16), [VMEM] * 6, 700_000_000)(
        rows, grad_out, balanced, place, late, weight
    )


def layer_output(rows, high, low, late_high, late_low):
    return call(output_kernel, shape((TOK_DEV, D), bf16), [VMEM] * 5, 4_000_000_000)(
        rows, high, low, late_high, late_low
    )


def partial_sum(terms):
    return call(part_kernel, shape((192, QUARTER), bf16), [VMEM], 1_000_000)(terms)


def last_sum(parts):
    return call(last_kernel, shape((4, D), f32), [VMEM], 1_000_000)(parts)


def shards(rollout, flows, route_ids, route_logits, grad_out, w_gate, w_up, w_down):
    ranks = lax.axis_size(DP)
    rank = lax.axis_index(DP).reshape(1)
    flows = flows.T
    head, tail, held, settle, place, late, weight, *shares = borders(
        rank, flows, rollout, route_ids.T, route_logits.T
    )
    left = lax.ppermute(tail, DP, [(i, (i + 1) % ranks) for i in range(ranks)])
    right = lax.ppermute(head, DP, [((i + 1) % ranks, i) for i in range(ranks)])
    outgoing, balanced = dispatch(left, right, held, settle, place, late)
    rows = exchange(outgoing, "fsdp", WIN)
    computed = ffn(rows, w_gate, w_up, w_down)
    returned = exchange(computed, "fsdp", WIN)
    terms = router_terms(returned, grad_out, balanced, place, late, weight)
    terms = exchange(terms, ("yl", "fsdp"), 64)
    layer_out = layer_output(returned, *shares)
    parts = exchange(partial_sum(terms), DP, 24)
    return (layer_out, last_sum(parts))


def solution(mesh):
    fine = Mesh(mesh.devices.reshape(2, 12, 32), ("yl", "z", "fsdp"))
    rows = P(("yl", "z", "fsdp"), None)
    expert = P("fsdp", None, None)
    return jax.shard_map(
        shards,
        mesh=fine,
        in_specs=(rows, P(None, "fsdp"), rows, rows, rows, expert, expert, expert),
        out_specs=(rows, P("fsdp", None)),
        check_vma=False,
    )
```

```python
import jax
import jax.numpy as jnp
from jax import lax
from jax.experimental import pallas as pl
from jax.experimental.pallas import tpu as pltpu
from jax.sharding import Mesh
from jax.sharding import PartitionSpec as P

D = 2048
HALF = D // 2
QUARTER = D // 4
FF = 768
EXPERTS = 128
WIN = 32
TOPK = 8
TOK_DEV = 128
SRC_DEV = 192
MOVE = 32
CAP = 12
SPAN = SRC_DEV + 2 * MOVE
WHOLE = 8
ROWS = WIN * WHOLE
WIDTH = D + HALF
SLOTS = WIN * CAP
BLOCK = 128
DP = ("yl", "z")
FF_CHUNK = 256
bf16, f32, i32 = jnp.bfloat16, jnp.float32, jnp.int32
VMEM = pl.BlockSpec(memory_space=pltpu.VMEM)
SMEM = pl.BlockSpec(memory_space=pltpu.SMEM)
HBM = pl.BlockSpec(memory_space=pltpu.HBM)


def iota(shape, dim):
    return lax.broadcasted_iota(i32, shape, dim)


def mm(a, b):
    return jnp.dot(a, b, preferred_element_type=f32)


def split2(v):
    high = v.astype(bf16)
    return high, (v - high.astype(f32)).astype(bf16)


def call(kernel, outs, in_specs, flops, scratch=(), limit=24 << 20):
    many = isinstance(outs, list)
    nbytes = sum(o.size * o.dtype.itemsize for o in (outs if many else [outs]))
    return pl.pallas_call(
        kernel,
        out_shape=outs,
        in_specs=in_specs,
        out_specs=[VMEM] * len(outs) if many else VMEM,
        scratch_shapes=list(scratch),
        cost_estimate=pl.CostEstimate(
            flops=flops, bytes_accessed=2 * nbytes, transcendentals=0
        ),
        compiler_params=pltpu.CompilerParams(vmem_limit_bytes=limit),
    )


def border_kernel(
    rank_ref,
    flows_hbm,
    rollout_hbm,
    ids_hbm,
    logits_hbm,
    head_ref,
    tail_ref,
    held_ref,
    settle_ref,
    place_ref,
    late_ref,
    weight_ref,
    high_ref,
    low_ref,
    late_high_ref,
    late_low_ref,
    flows,
    ids,
    logits,
    sems,
):
    flow_copy = pltpu.make_async_copy(flows_hbm, flows, sems.at[0])
    ids_copy = pltpu.make_async_copy(ids_hbm, ids, sems.at[1])
    logits_copy = pltpu.make_async_copy(logits_hbm, logits, sems.at[2])
    held_copy = pltpu.make_async_copy(rollout_hbm, held_ref, sems.at[3])
    flow_copy.start()
    ids_copy.start()
    logits_copy.start()
    held_copy.start()
    ids_copy.wait()
    logits_copy.wait()
    route(
        ids,
        logits[...],
        place_ref,
        late_ref,
        weight_ref,
        (high_ref, low_ref),
        (late_high_ref, late_low_ref),
    )
    flow_copy.wait()
    rank = rank_ref[0]
    left = flows[0, jnp.where(rank == 0, 23, rank - 1)]
    live = TOK_DEV + flows[0, rank] - left
    at = iota((TOK_DEV, SPAN), 0) + (MOVE - left)
    at = jnp.where(at < MOVE + live, at, at + (SRC_DEV - live))
    settle_ref[...] = (iota((TOK_DEV, SPAN), 1) == at).astype(bf16)
    at = iota((MOVE, SRC_DEV), 0) + (live - MOVE)
    pick = (iota((MOVE, SRC_DEV), 1) == at).astype(bf16)
    held_copy.wait()
    head_ref[...] = held_ref[:MOVE, :]
    tail_ref[...] = mm(pick, held_ref[...]).astype(bf16)


def route(ids, logits, place_ref, late_ref, weight_ref, parts_refs, late_parts_refs):
    raised = jnp.exp(logits - jnp.max(logits, axis=0, keepdims=True))
    share = raised / jnp.sum(raised, axis=0, keepdims=True)
    expert = iota((EXPERTS, TOK_DEV), 0)
    weight = jnp.zeros((EXPERTS, TOK_DEV), f32)
    named = jnp.zeros((EXPERTS, TOK_DEV), f32)
    for k in range(TOPK):
        hit = ids[k : k + 1, :] == expert
        weight = jnp.where(hit, share[k : k + 1, :], weight)
        named = jnp.where(hit, 1.0, named)
    weight_ref[...] = weight
    upto = (iota((TOK_DEV, TOK_DEV), 0) <= iota((TOK_DEV, TOK_DEV), 1)).astype(bf16)
    count = mm(named[:WIN].astype(bf16), upto)
    code = jnp.where(named[:WIN] > 0.0, count, 0.0).astype(bf16)
    spread = ((iota((ROWS, WIN), 0) >> 3) == iota((ROWS, WIN), 1)).astype(bf16)
    row = iota((ROWS, TOK_DEV), 0)
    codes = mm(spread, code).astype(i32)
    whole = codes == (row & 7) + 1
    late = codes == (row & 3) + (WHOLE + 1)
    second = (row & 4) == 4
    place_ref[...] = whole.astype(bf16)
    for half in range(2):
        cols = slice(half * TOK_DEV, (half + 1) * TOK_DEV)
        late_ref[:, cols] = (late & (second == (half == 1))).astype(bf16)
    for part, out, late_out in zip(split2(weight[:WIN]), parts_refs, late_parts_refs):
        spreads = mm(spread, part)
        out[...] = jnp.where(whole, spreads, 0.0).T.astype(bf16)
        for half in range(2):
            mine = late & (second == (half == 1))
            late_out[half * TOK_DEV : (half + 1) * TOK_DEV, :] = (
                jnp.where(mine, spreads, 0.0).T.astype(bf16)
            )


def halves(wide):
    return jnp.concatenate([wide[:, :HALF], wide[:, HALF:]], axis=0)


def dispatch_kernel(
    left_ref, right_ref, held_ref, settle_ref, place_ref, late_ref, out_ref, bal_ref
):
    rows = jnp.concatenate([left_ref[...], held_ref[...], right_ref[...]], axis=0)
    balanced = mm(settle_ref[...], rows).astype(bf16)
    bal_ref[...] = balanced
    out_ref[:, :D] = mm(place_ref[...], balanced).astype(bf16)
    out_ref[:, D:] = mm(late_ref[...], halves(balanced)).astype(bf16)


def block_source(dim):
    row = iota((BLOCK, BLOCK), dim)
    return ((row >> 2) & 15) * 8 + (row >> 6) * 4 + (row & 3)


def ffn_kernel(rows_ref, gate_ref, up_ref, down_ref, out_ref, x, hidden):
    ordered = (iota((BLOCK, BLOCK), 1) == block_source(0)).astype(bf16)
    back = (iota((BLOCK, BLOCK), 0) == block_source(1)).astype(bf16)
    part_rows = BLOCK // 2
    x[:ROWS, :] = rows_ref[:, :D]
    for b in range(ROWS // BLOCK):
        y = mm(ordered, rows_ref[b * BLOCK : (b + 1) * BLOCK, D:]).astype(bf16)
        mine = slice(ROWS + b * part_rows, ROWS + (b + 1) * part_rows)
        x[mine, :HALF] = y[:part_rows]
        x[mine, HALF:] = y[part_rows:]
    for f in range(FF // FF_CHUNK):
        cols = slice(f * FF_CHUNK, (f + 1) * FF_CHUNK)
        g = mm(x[...], gate_ref[0, :, cols])
        u = mm(x[...], up_ref[0, :, cols])
        hidden[:, cols] = (g / (1.0 + jnp.exp(-g)) * u).astype(bf16)
    late = []
    for half in range(2):
        cols = slice(half * HALF, (half + 1) * HALF)
        y = mm(hidden[...], down_ref[0, :, cols]).astype(bf16)
        out_ref[:, cols] = y[:ROWS]
        late.append(y[ROWS:])
    for b in range(ROWS // BLOCK):
        mine = slice(b * part_rows, (b + 1) * part_rows)
        y = jnp.concatenate([late[0][mine], late[1][mine]], axis=0)
        out_ref[b * BLOCK : (b + 1) * BLOCK, D:] = mm(back, y).astype(bf16)


def against(a, b):
    return lax.dot_general(a, b, (((1,), (1,)), ((), ())), preferred_element_type=f32)


def terms_kernel(rows_ref, grad_ref, bal_ref, place_ref, late_ref, weight_ref, out_ref):
    cotangent = grad_ref[...]
    scores = against(rows_ref[:, :D], cotangent) * place_ref[...].astype(f32)
    late = against(rows_ref[:, D:], halves(cotangent)) * late_ref[...].astype(f32)
    scores = scores + late[:, :TOK_DEV] + late[:, TOK_DEV:]
    score = jnp.sum(scores.reshape(WIN, WHOLE, TOK_DEV), axis=1)
    weight = weight_ref[...]
    total = jnp.sum(weight[:WIN] * score, axis=0, keepdims=True)
    grad = jnp.concatenate(
        [weight[:WIN] * (score - total), weight[WIN:] * (0.0 - total)], axis=0
    )
    high, low = split2(grad)
    line = iota((2 * EXPERTS, EXPERTS), 0)
    order = (iota((2 * EXPERTS, EXPERTS), 1) == (line >> 3) * 4 + (line & 3)).astype(bf16)
    factor = jnp.concatenate(
        [mm(order, high).astype(bf16), mm(order, low).astype(bf16)], axis=1
    )
    first = (iota((2 * EXPERTS, QUARTER), 0) & 4) == 0
    for half in range(2):
        tokens = bal_ref[:, half * HALF : (half + 1) * HALF]
        term = mm(factor, jnp.concatenate([tokens, tokens], axis=0))
        out_ref[half * 2 * EXPERTS : (half + 1) * 2 * EXPERTS, :] = jnp.where(
            first, term[:, :QUARTER], term[:, QUARTER:]
        ).astype(bf16)


def output_kernel(rows_ref, high_ref, low_ref, late_high_ref, late_low_ref, out_ref):
    rows, ends = rows_ref[:, :D], rows_ref[:, D:]
    late = mm(late_high_ref[...], ends) + mm(late_low_ref[...], ends)
    both = mm(high_ref[...], rows) + mm(low_ref[...], rows)
    out_ref[:, :HALF] = (both[:, :HALF] + late[:TOK_DEV]).astype(bf16)
    out_ref[:, HALF:] = (both[:, HALF:] + late[TOK_DEV:]).astype(bf16)


def part_kernel(terms_ref, out_ref):
    part = jnp.sum(terms_ref[...].astype(f32).reshape(64, 8, QUARTER), axis=0)
    two = jnp.concatenate([part, part], axis=0).astype(bf16)
    for i in range(12):
        out_ref[16 * i : 16 * (i + 1), :] = two


def last_kernel(parts_ref, out_ref):
    parts = jnp.sum(parts_ref[...].astype(f32).reshape(2, 12, 8, QUARTER), axis=1)
    for half in range(2):
        for quarter in range(2):
            at = half * HALF + quarter * QUARTER
            out_ref[:, at : at + QUARTER] = parts[half, 4 * quarter : 4 * quarter + 4]


def in_hbm(array):
    return pltpu.with_memory_space_constraint(array, pltpu.HBM)


def shape(dims, dtype):
    return jax.ShapeDtypeStruct(dims, dtype)


def exchange(blocks, axes, peers):
    rows, cols = blocks.shape
    apart = blocks.reshape(peers, rows // peers, cols)
    return lax.all_to_all(apart, axes, split_axis=0, concat_axis=0, tiled=True).reshape(rows, cols)


def borders(rank, flows, rollout, ids, logits):
    return call(
        border_kernel,
        [
            shape((MOVE, D), bf16),
            shape((MOVE, D), bf16),
            shape((SRC_DEV, D), bf16),
            shape((TOK_DEV, SPAN), bf16),
            shape((ROWS, TOK_DEV), bf16),
            shape((ROWS, 2 * TOK_DEV), bf16),
            shape((EXPERTS, TOK_DEV), f32),
            shape((TOK_DEV, ROWS), bf16),
            shape((TOK_DEV, ROWS), bf16),
            shape((2 * TOK_DEV, ROWS), bf16),
            shape((2 * TOK_DEV, ROWS), bf16),
        ],
        [SMEM] + [HBM] * 4,
        25_000_000,
        [
            pltpu.SMEM((1, 24), i32),
            pltpu.VMEM((TOPK, TOK_DEV), i32),
            pltpu.VMEM((TOPK, TOK_DEV), f32),
            pltpu.SemaphoreType.DMA((4,)),
        ],
    )(rank, *[in_hbm(v) for v in (flows, rollout, ids, logits)])


def dispatch(left, right, held, settle, place, late):
    return call(
        dispatch_kernel,
        [shape((ROWS, WIDTH), bf16), shape((TOK_DEV, D), bf16)],
        [VMEM] * 6,
        12_000_000_000,
    )(left, right, held, settle, place, late)


def ffn(rows, w_gate, w_up, w_down):
    return call(
        ffn_kernel,
        shape((ROWS, WIDTH), bf16),
        [VMEM] * 4,
        3_700_000_000,
        [pltpu.VMEM((SLOTS, D), bf16), pltpu.VMEM((SLOTS, FF), bf16)],
    )(rows, w_gate, w_up, w_down)


def router_terms(rows, grad_out, balanced, place, late, weight):
    return call(terms_kernel, shape((4 * EXPERTS, QUARTER), bf16), [VMEM] * 6, 700_000_000)(
        rows, grad_out, balanced, place, late, weight
    )


def layer_output(rows, high, low, late_high, late_low):
    return call(output_kernel, shape((TOK_DEV, D), bf16), [VMEM] * 5, 4_000_000_000)(
        rows, high, low, late_high, late_low
    )


def partial_sum(terms):
    return call(part_kernel, shape((192, QUARTER), bf16), [VMEM], 1_000_000)(terms)


def last_sum(parts):
    return call(last_kernel, shape((4, D), f32), [VMEM], 1_000_000)(parts)


def shards(rollout, flows, route_ids, route_logits, grad_out, w_gate, w_up, w_down):
    ranks = lax.axis_size(DP)
    rank = lax.axis_index(DP).reshape(1)
    flows = flows.T
    head, tail, held, settle, place, late, weight, *shares = borders(
        rank, flows, rollout, route_ids.T, route_logits.T
    )
    left = lax.ppermute(tail, DP, [(i, (i + 1) % ranks) for i in range(ranks)])
    right = lax.ppermute(head, DP, [((i + 1) % ranks, i) for i in range(ranks)])
    outgoing, balanced = dispatch(left, right, held, settle, place, late)
    rows = exchange(outgoing, "fsdp", WIN)
    computed = ffn(rows, w_gate, w_up, w_down)
    returned = exchange(computed, "fsdp", WIN)
    terms = router_terms(returned, grad_out, balanced, place, late, weight)
    terms = exchange(terms, ("yl", "fsdp"), 64)
    layer_out = layer_output(returned, *shares)
    parts = exchange(partial_sum(terms), DP, 24)
    return (layer_out, last_sum(parts))


def solution(mesh):
    fine = Mesh(mesh.devices.reshape(2, 12, 32), ("yl", "z", "fsdp"))
    rows = P(("yl", "z", "fsdp"), None)
    expert = P("fsdp", None, None)
    return jax.shard_map(
        shards,
        mesh=fine,
        in_specs=(rows, P(None, "fsdp"), rows, rows, rows, expert, expert, expert),
        out_specs=(rows, P("fsdp", None)),
        check_vma=False,
    )
```

```python
import jax
import jax.numpy as jnp
from jax import lax
from jax.experimental import pallas as pl
from jax.experimental.pallas import tpu as pltpu
from jax.sharding import Mesh
from jax.sharding import PartitionSpec as P

D = 2048
HALF = D // 2
QUARTER = D // 4
FF = 768
EXPERTS = 128
WIN = 32
TOPK = 8
TOK_DEV = 128
SRC_DEV = 192
MOVE = 32
CAP = 12
SPAN = SRC_DEV + 2 * MOVE
WHOLE = 8
ROWS = WIN * WHOLE
WIDTH = D + HALF
SLOTS = WIN * CAP
BLOCK = 128
DP = ("yl", "z")
FSDP = ("chip", "core")
CHIPS = 16
FF_CHUNK = 256
bf16, f32, i32 = jnp.bfloat16, jnp.float32, jnp.int32
VMEM = pl.BlockSpec(memory_space=pltpu.VMEM)
SMEM = pl.BlockSpec(memory_space=pltpu.SMEM)
HBM = pl.BlockSpec(memory_space=pltpu.HBM)


def iota(shape, dim):
    return lax.broadcasted_iota(i32, shape, dim)


def mm(a, b):
    return jnp.dot(a, b, preferred_element_type=f32)


def split2(v):
    high = v.astype(bf16)
    return high, (v - high.astype(f32)).astype(bf16)


def call(kernel, outs, in_specs, flops, scratch=(), limit=24 << 20):
    many = isinstance(outs, list)
    nbytes = sum(o.size * o.dtype.itemsize for o in (outs if many else [outs]))
    return pl.pallas_call(
        kernel,
        out_shape=outs,
        in_specs=in_specs,
        out_specs=[VMEM] * len(outs) if many else VMEM,
        scratch_shapes=list(scratch),
        cost_estimate=pl.CostEstimate(
            flops=flops, bytes_accessed=2 * nbytes, transcendentals=0
        ),
        compiler_params=pltpu.CompilerParams(vmem_limit_bytes=limit),
    )


def border_kernel(
    rank_ref,
    core_ref,
    flows_hbm,
    rollout_hbm,
    ids_hbm,
    logits_hbm,
    head_ref,
    tail_ref,
    held_ref,
    settle_ref,
    order_ref,
    place_ref,
    late_ref,
    weight_ref,
    high_ref,
    low_ref,
    late_high_ref,
    late_low_ref,
    flows,
    ids,
    logits,
    sems,
):
    flow_copy = pltpu.make_async_copy(flows_hbm, flows, sems.at[0])
    ids_copy = pltpu.make_async_copy(ids_hbm, ids, sems.at[1])
    logits_copy = pltpu.make_async_copy(logits_hbm, logits, sems.at[2])
    held_copy = pltpu.make_async_copy(rollout_hbm, held_ref, sems.at[3])
    flow_copy.start()
    ids_copy.start()
    logits_copy.start()
    held_copy.start()
    ids_copy.wait()
    logits_copy.wait()
    route(
        ids,
        logits[...],
        place_ref,
        late_ref,
        weight_ref,
        (high_ref, low_ref),
        (late_high_ref, late_low_ref),
    )
    line = iota((2 * EXPERTS, EXPERTS), 0)
    core = jnp.where(line < EXPERTS, core_ref[0], 1 - core_ref[0])
    expert = ((line >> 3) & 15) * 8 + 4 * core + (line & 3)
    order_ref[...] = (iota((2 * EXPERTS, EXPERTS), 1) == expert).astype(bf16)
    flow_copy.wait()
    rank = rank_ref[0]
    left = flows[0, jnp.where(rank == 0, 23, rank - 1)]
    live = TOK_DEV + flows[0, rank] - left
    at = iota((TOK_DEV, SPAN), 0) + (MOVE - left)
    at = jnp.where(at < MOVE + live, at, at + (SRC_DEV - live))
    settle_ref[...] = (iota((TOK_DEV, SPAN), 1) == at).astype(bf16)
    at = iota((MOVE, SRC_DEV), 0) + (live - MOVE)
    pick = (iota((MOVE, SRC_DEV), 1) == at).astype(bf16)
    held_copy.wait()
    head_ref[...] = held_ref[:MOVE, :]
    tail_ref[...] = mm(pick, held_ref[...]).astype(bf16)


def route(ids, logits, place_ref, late_ref, weight_ref, parts_refs, late_parts_refs):
    raised = jnp.exp(logits - jnp.max(logits, axis=0, keepdims=True))
    share = raised / jnp.sum(raised, axis=0, keepdims=True)
    expert = iota((EXPERTS, TOK_DEV), 0)
    weight = jnp.zeros((EXPERTS, TOK_DEV), f32)
    named = jnp.zeros((EXPERTS, TOK_DEV), f32)
    for k in range(TOPK):
        hit = ids[k : k + 1, :] == expert
        weight = jnp.where(hit, share[k : k + 1, :], weight)
        named = jnp.where(hit, 1.0, named)
    weight_ref[...] = weight
    upto = (iota((TOK_DEV, TOK_DEV), 0) <= iota((TOK_DEV, TOK_DEV), 1)).astype(bf16)
    count = mm(named[:WIN].astype(bf16), upto)
    code = jnp.where(named[:WIN] > 0.0, count, 0.0).astype(bf16)
    spread = ((iota((ROWS, WIN), 0) >> 3) == iota((ROWS, WIN), 1)).astype(bf16)
    row = iota((ROWS, TOK_DEV), 0)
    codes = mm(spread, code).astype(i32)
    whole = codes == (row & 7) + 1
    late = codes == (row & 3) + (WHOLE + 1)
    second = (row & 4) == 4
    place_ref[...] = whole.astype(bf16)
    for half in range(2):
        cols = slice(half * TOK_DEV, (half + 1) * TOK_DEV)
        late_ref[:, cols] = (late & (second == (half == 1))).astype(bf16)
    for part, out, late_out in zip(split2(weight[:WIN]), parts_refs, late_parts_refs):
        spreads = mm(spread, part)
        out[...] = jnp.where(whole, spreads, 0.0).T.astype(bf16)
        for half in range(2):
            mine = late & (second == (half == 1))
            late_out[half * TOK_DEV : (half + 1) * TOK_DEV, :] = (
                jnp.where(mine, spreads, 0.0).T.astype(bf16)
            )


def halves(wide):
    return jnp.concatenate([wide[:, :HALF], wide[:, HALF:]], axis=0)


def dispatch_kernel(
    left_ref, right_ref, held_ref, settle_ref, place_ref, late_ref, out_ref, bal_ref
):
    rows = jnp.concatenate([left_ref[...], held_ref[...], right_ref[...]], axis=0)
    balanced = mm(settle_ref[...], rows).astype(bf16)
    bal_ref[...] = balanced
    out_ref[:, :D] = mm(place_ref[...], balanced).astype(bf16)
    out_ref[:, D:] = mm(late_ref[...], halves(balanced)).astype(bf16)


def block_source(dim):
    row = iota((BLOCK, BLOCK), dim)
    return ((row >> 2) & 15) * 8 + (row >> 6) * 4 + (row & 3)


def ffn_kernel(rows_ref, gate_ref, up_ref, down_ref, out_ref, x, hidden):
    ordered = (iota((BLOCK, BLOCK), 1) == block_source(0)).astype(bf16)
    back = (iota((BLOCK, BLOCK), 0) == block_source(1)).astype(bf16)
    part_rows = BLOCK // 2
    x[:ROWS, :] = rows_ref[:, :D]
    for b in range(ROWS // BLOCK):
        y = mm(ordered, rows_ref[b * BLOCK : (b + 1) * BLOCK, D:]).astype(bf16)
        mine = slice(ROWS + b * part_rows, ROWS + (b + 1) * part_rows)
        x[mine, :HALF] = y[:part_rows]
        x[mine, HALF:] = y[part_rows:]
    for f in range(FF // FF_CHUNK):
        cols = slice(f * FF_CHUNK, (f + 1) * FF_CHUNK)
        g = mm(x[...], gate_ref[0, :, cols])
        u = mm(x[...], up_ref[0, :, cols])
        hidden[:, cols] = (g / (1.0 + jnp.exp(-g)) * u).astype(bf16)
    late = []
    for half in range(2):
        cols = slice(half * HALF, (half + 1) * HALF)
        y = mm(hidden[...], down_ref[0, :, cols]).astype(bf16)
        out_ref[:, cols] = y[:ROWS]
        late.append(y[ROWS:])
    for b in range(ROWS // BLOCK):
        mine = slice(b * part_rows, (b + 1) * part_rows)
        y = jnp.concatenate([late[0][mine], late[1][mine]], axis=0)
        out_ref[b * BLOCK : (b + 1) * BLOCK, D:] = mm(back, y).astype(bf16)


def against(a, b):
    return lax.dot_general(a, b, (((1,), (1,)), ((), ())), preferred_element_type=f32)


def terms_kernel(
    rows_ref,
    grad_ref,
    bal_ref,
    order_ref,
    place_ref,
    late_ref,
    weight_ref,
    other_ref,
    factor_ref,
):
    cotangent = grad_ref[...]
    scores = against(rows_ref[:, :D], cotangent) * place_ref[...].astype(f32)
    late = against(rows_ref[:, D:], halves(cotangent)) * late_ref[...].astype(f32)
    scores = scores + late[:, :TOK_DEV] + late[:, TOK_DEV:]
    score = jnp.sum(scores.reshape(WIN, WHOLE, TOK_DEV), axis=1)
    weight = weight_ref[...]
    total = jnp.sum(weight[:WIN] * score, axis=0, keepdims=True)
    grad = jnp.concatenate(
        [weight[:WIN] * (score - total), weight[WIN:] * (0.0 - total)], axis=0
    )
    high, low = split2(grad)
    factor = jnp.concatenate(
        [mm(order_ref[...], high).astype(bf16), mm(order_ref[...], low).astype(bf16)], axis=1
    )
    factor_ref[...] = factor[:EXPERTS]
    for half in range(2):
        other_ref[half * EXPERTS : (half + 1) * EXPERTS, :] = half_terms(
            factor[EXPERTS:], bal_ref, half
        ).astype(bf16)


def half_terms(factor, bal_ref, half):
    tokens = bal_ref[:, half * HALF : (half + 1) * HALF]
    term = mm(factor, jnp.concatenate([tokens, tokens], axis=0))
    first = (iota((EXPERTS, QUARTER), 0) & 4) == 0
    return jnp.where(first, term[:, :QUARTER], term[:, QUARTER:])


def join_kernel(factor_ref, bal_ref, given_ref, out_ref):
    for half in range(2):
        rows = slice(half * EXPERTS, (half + 1) * EXPERTS)
        own = half_terms(factor_ref[...], bal_ref, half)
        out_ref[rows, :] = (own + given_ref[rows, :].astype(f32)).astype(bf16)


def output_kernel(rows_ref, high_ref, low_ref, late_high_ref, late_low_ref, out_ref):
    rows, ends = rows_ref[:, :D], rows_ref[:, D:]
    late = mm(late_high_ref[...], ends) + mm(late_low_ref[...], ends)
    both = mm(high_ref[...], rows) + mm(low_ref[...], rows)
    out_ref[:, :HALF] = (both[:, :HALF] + late[:TOK_DEV]).astype(bf16)
    out_ref[:, HALF:] = (both[:, HALF:] + late[TOK_DEV:]).astype(bf16)


def part_kernel(terms_ref, out_ref):
    part = jnp.sum(terms_ref[...].astype(f32).reshape(2 * CHIPS, 8, QUARTER), axis=0)
    two = jnp.concatenate([part, part], axis=0).astype(bf16)
    for i in range(12):
        out_ref[16 * i : 16 * (i + 1), :] = two


def last_kernel(parts_ref, out_ref):
    parts = jnp.sum(parts_ref[...].astype(f32).reshape(2, 12, 8, QUARTER), axis=1)
    for half in range(2):
        for quarter in range(2):
            at = half * HALF + quarter * QUARTER
            out_ref[:, at : at + QUARTER] = parts[half, 4 * quarter : 4 * quarter + 4]


def in_hbm(array):
    return pltpu.with_memory_space_constraint(array, pltpu.HBM)


def shape(dims, dtype):
    return jax.ShapeDtypeStruct(dims, dtype)


def exchange(blocks, axes, peers):
    rows, cols = blocks.shape
    apart = blocks.reshape(peers, rows // peers, cols)
    return lax.all_to_all(apart, axes, split_axis=0, concat_axis=0, tiled=True).reshape(rows, cols)


def borders(rank, core, flows, rollout, ids, logits):
    return call(
        border_kernel,
        [
            shape((MOVE, D), bf16),
            shape((MOVE, D), bf16),
            shape((SRC_DEV, D), bf16),
            shape((TOK_DEV, SPAN), bf16),
            shape((2 * EXPERTS, EXPERTS), bf16),
            shape((ROWS, TOK_DEV), bf16),
            shape((ROWS, 2 * TOK_DEV), bf16),
            shape((EXPERTS, TOK_DEV), f32),
            shape((TOK_DEV, ROWS), bf16),
            shape((TOK_DEV, ROWS), bf16),
            shape((2 * TOK_DEV, ROWS), bf16),
            shape((2 * TOK_DEV, ROWS), bf16),
        ],
        [SMEM] * 2 + [HBM] * 4,
        25_000_000,
        [
            pltpu.SMEM((1, 24), i32),
            pltpu.VMEM((TOPK, TOK_DEV), i32),
            pltpu.VMEM((TOPK, TOK_DEV), f32),
            pltpu.SemaphoreType.DMA((4,)),
        ],
    )(rank, core, *[in_hbm(v) for v in (flows, rollout, ids, logits)])


def dispatch(left, right, held, settle, place, late):
    return call(
        dispatch_kernel,
        [shape((ROWS, WIDTH), bf16), shape((TOK_DEV, D), bf16)],
        [VMEM] * 6,
        12_000_000_000,
    )(left, right, held, settle, place, late)


def ffn(rows, w_gate, w_up, w_down):
    return call(
        ffn_kernel,
        shape((ROWS, WIDTH), bf16),
        [VMEM] * 4,
        3_700_000_000,
        [pltpu.VMEM((SLOTS, D), bf16), pltpu.VMEM((SLOTS, FF), bf16)],
    )(rows, w_gate, w_up, w_down)


def router_terms(rows, grad_out, balanced, order, place, late, weight):
    return call(
        terms_kernel,
        [shape((2 * EXPERTS, QUARTER), bf16), shape((EXPERTS, 2 * TOK_DEV), bf16)],
        [VMEM] * 7,
        500_000_000,
    )(rows, grad_out, balanced, order, place, late, weight)


def join(factor, balanced, given):
    return call(join_kernel, shape((2 * EXPERTS, QUARTER), bf16), [VMEM] * 3, 150_000_000)(
        factor, balanced, given
    )


def layer_output(rows, high, low, late_high, late_low):
    return call(output_kernel, shape((TOK_DEV, D), bf16), [VMEM] * 5, 4_000_000_000)(
        rows, high, low, late_high, late_low
    )


def partial_sum(terms):
    return call(part_kernel, shape((192, QUARTER), bf16), [VMEM], 1_000_000)(terms)


def last_sum(parts):
    return call(last_kernel, shape((4, D), f32), [VMEM], 1_000_000)(parts)


def shards(rollout, flows, route_ids, route_logits, grad_out, w_gate, w_up, w_down):
    ranks = lax.axis_size(DP)
    rank = lax.axis_index(DP).reshape(1)
    core = lax.axis_index("core").reshape(1)
    flows = flows.T
    head, tail, held, settle, order, place, late, weight, *shares = borders(
        rank, core, flows, rollout, route_ids.T, route_logits.T
    )
    left = lax.ppermute(tail, DP, [(i, (i + 1) % ranks) for i in range(ranks)])
    right = lax.ppermute(head, DP, [((i + 1) % ranks, i) for i in range(ranks)])
    outgoing, balanced = dispatch(left, right, held, settle, place, late)
    rows = exchange(outgoing, FSDP, WIN)
    computed = ffn(rows, w_gate, w_up, w_down)
    returned = exchange(computed, FSDP, WIN)
    other, factor = router_terms(returned, grad_out, balanced, order, place, late, weight)
    given = lax.ppermute(other, "core", [(0, 1), (1, 0)])
    terms = exchange(join(factor, balanced, given), ("yl", "chip"), 2 * CHIPS)
    layer_out = layer_output(returned, *shares)
    parts = exchange(partial_sum(terms), DP, 24)
    return (layer_out, last_sum(parts))


def solution(mesh):
    fine = Mesh(mesh.devices.reshape(2, 12, CHIPS, 2), DP + FSDP)
    rows = P(DP + FSDP, None)
    expert = P(FSDP, None, None)
    return jax.shard_map(
        shards,
        mesh=fine,
        in_specs=(rows, P(None, FSDP), rows, rows, rows, expert, expert, expert),
        out_specs=(rows, P(FSDP, None)),
        check_vma=False,
    )
```

```python
import jax
import jax.numpy as jnp
from jax import lax
from jax.experimental import pallas as pl
from jax.experimental.pallas import tpu as pltpu
from jax.sharding import Mesh
from jax.sharding import PartitionSpec as P

D = 2048
HALF = D // 2
QUARTER = D // 4
FF = 768
EXPERTS = 128
WIN = 32
TOPK = 8
TOK_DEV = 128
SRC_DEV = 192
MOVE = 32
CAP = 12
SPAN = SRC_DEV + 2 * MOVE
WHOLE = 8
ROWS = WIN * WHOLE
WIDTH = D + HALF
SLOTS = WIN * CAP
BLOCK = 128
DP = ("yl", "z")
FSDP = ("chip", "core")
CHIPS = 16
FF_CHUNK = 256
bf16, f32, i32 = jnp.bfloat16, jnp.float32, jnp.int32
VMEM = pl.BlockSpec(memory_space=pltpu.VMEM)
SMEM = pl.BlockSpec(memory_space=pltpu.SMEM)
HBM = pl.BlockSpec(memory_space=pltpu.HBM)


def iota(shape, dim):
    return lax.broadcasted_iota(i32, shape, dim)


def mm(a, b):
    return jnp.dot(a, b, preferred_element_type=f32)


def split2(v):
    high = v.astype(bf16)
    return high, (v - high.astype(f32)).astype(bf16)


def call(kernel, outs, in_specs, flops, scratch=(), limit=24 << 20):
    many = isinstance(outs, list)
    nbytes = sum(o.size * o.dtype.itemsize for o in (outs if many else [outs]))
    return pl.pallas_call(
        kernel,
        out_shape=outs,
        in_specs=in_specs,
        out_specs=[VMEM] * len(outs) if many else VMEM,
        scratch_shapes=list(scratch),
        cost_estimate=pl.CostEstimate(
            flops=flops, bytes_accessed=2 * nbytes, transcendentals=0
        ),
        compiler_params=pltpu.CompilerParams(vmem_limit_bytes=limit),
    )


def border_kernel(
    rank_ref,
    core_ref,
    flows_hbm,
    rollout_hbm,
    ids_hbm,
    logits_hbm,
    head_ref,
    tail_ref,
    held_ref,
    settle_ref,
    order_ref,
    place_ref,
    late_ref,
    weight_ref,
    high_ref,
    low_ref,
    late_high_ref,
    late_low_ref,
    flows,
    ids,
    logits,
    sems,
):
    flow_copy = pltpu.make_async_copy(flows_hbm, flows, sems.at[0])
    ids_copy = pltpu.make_async_copy(ids_hbm, ids, sems.at[1])
    logits_copy = pltpu.make_async_copy(logits_hbm, logits, sems.at[2])
    held_copy = pltpu.make_async_copy(rollout_hbm, held_ref, sems.at[3])
    flow_copy.start()
    ids_copy.start()
    logits_copy.start()
    held_copy.start()
    ids_copy.wait()
    logits_copy.wait()
    route(
        ids,
        logits[...],
        place_ref,
        late_ref,
        weight_ref,
        (high_ref, low_ref),
        (late_high_ref, late_low_ref),
    )
    line = iota((2 * EXPERTS, EXPERTS), 0)
    core = jnp.where(line < EXPERTS, core_ref[0], 1 - core_ref[0])
    expert = ((line >> 3) & 15) * 8 + 4 * core + (line & 3)
    order_ref[...] = (iota((2 * EXPERTS, EXPERTS), 1) == expert).astype(bf16)
    flow_copy.wait()
    rank = rank_ref[0]
    left = flows[0, jnp.where(rank == 0, 23, rank - 1)]
    live = TOK_DEV + flows[0, rank] - left
    at = iota((TOK_DEV, SPAN), 0) + (MOVE - left)
    at = jnp.where(at < MOVE + live, at, at + (SRC_DEV - live))
    settle_ref[...] = (iota((TOK_DEV, SPAN), 1) == at).astype(bf16)
    at = iota((MOVE, SRC_DEV), 0) + (live - MOVE)
    pick = (iota((MOVE, SRC_DEV), 1) == at).astype(bf16)
    held_copy.wait()
    head_ref[...] = held_ref[:MOVE, :]
    tail_ref[...] = mm(pick, held_ref[...]).astype(bf16)


def route(ids, logits, place_ref, late_ref, weight_ref, parts_refs, late_parts_refs):
    raised = jnp.exp(logits - jnp.max(logits, axis=0, keepdims=True))
    share = raised / jnp.sum(raised, axis=0, keepdims=True)
    expert = iota((EXPERTS, TOK_DEV), 0)
    weight = jnp.zeros((EXPERTS, TOK_DEV), f32)
    named = jnp.zeros((EXPERTS, TOK_DEV), f32)
    for k in range(TOPK):
        hit = ids[k : k + 1, :] == expert
        weight = jnp.where(hit, share[k : k + 1, :], weight)
        named = jnp.where(hit, 1.0, named)
    weight_ref[...] = weight
    upto = (iota((TOK_DEV, TOK_DEV), 0) <= iota((TOK_DEV, TOK_DEV), 1)).astype(bf16)
    count = mm(named[:WIN].astype(bf16), upto)
    code = jnp.where(named[:WIN] > 0.0, count, 0.0).astype(bf16)
    spread = ((iota((ROWS, WIN), 0) >> 3) == iota((ROWS, WIN), 1)).astype(bf16)
    row = iota((ROWS, TOK_DEV), 0)
    codes = mm(spread, code).astype(i32)
    whole = codes == (row & 7) + 1
    late = codes == (row & 3) + (WHOLE + 1)
    second = (row & 4) == 4
    place_ref[...] = whole.astype(bf16)
    for half in range(2):
        cols = slice(half * TOK_DEV, (half + 1) * TOK_DEV)
        late_ref[:, cols] = (late & (second == (half == 1))).astype(bf16)
    for part, out, late_out in zip(split2(weight[:WIN]), parts_refs, late_parts_refs):
        spreads = mm(spread, part)
        out[...] = jnp.where(whole, spreads, 0.0).T.astype(bf16)
        for half in range(2):
            mine = late & (second == (half == 1))
            late_out[half * TOK_DEV : (half + 1) * TOK_DEV, :] = (
                jnp.where(mine, spreads, 0.0).T.astype(bf16)
            )


def halves(wide):
    return jnp.concatenate([wide[:, :HALF], wide[:, HALF:]], axis=0)


def dispatch_kernel(
    left_ref, right_ref, held_ref, settle_ref, place_ref, late_ref, out_ref, bal_ref
):
    rows = jnp.concatenate([left_ref[...], held_ref[...], right_ref[...]], axis=0)
    balanced = mm(settle_ref[...], rows).astype(bf16)
    bal_ref[...] = balanced
    out_ref[:, :D] = mm(place_ref[...], balanced).astype(bf16)
    out_ref[:, D:] = mm(late_ref[...], halves(balanced)).astype(bf16)


def block_source(dim):
    row = iota((BLOCK, BLOCK), dim)
    return ((row >> 2) & 15) * 8 + (row >> 6) * 4 + (row & 3)


def ffn_kernel(rows_ref, gate_ref, up_ref, down_ref, out_ref, x, hidden):
    ordered = (iota((BLOCK, BLOCK), 1) == block_source(0)).astype(bf16)
    back = (iota((BLOCK, BLOCK), 0) == block_source(1)).astype(bf16)
    part_rows = BLOCK // 2
    x[:ROWS, :] = rows_ref[:, :D]
    for b in range(ROWS // BLOCK):
        y = mm(ordered, rows_ref[b * BLOCK : (b + 1) * BLOCK, D:]).astype(bf16)
        mine = slice(ROWS + b * part_rows, ROWS + (b + 1) * part_rows)
        x[mine, :HALF] = y[:part_rows]
        x[mine, HALF:] = y[part_rows:]
    for f in range(FF // FF_CHUNK):
        cols = slice(f * FF_CHUNK, (f + 1) * FF_CHUNK)
        g = mm(x[...], gate_ref[0, :, cols])
        u = mm(x[...], up_ref[0, :, cols])
        hidden[:, cols] = (g / (1.0 + jnp.exp(-g)) * u).astype(bf16)
    late = []
    for half in range(2):
        cols = slice(half * HALF, (half + 1) * HALF)
        y = mm(hidden[...], down_ref[0, :, cols]).astype(bf16)
        out_ref[:, cols] = y[:ROWS]
        late.append(y[ROWS:])
    for b in range(ROWS // BLOCK):
        mine = slice(b * part_rows, (b + 1) * part_rows)
        y = jnp.concatenate([late[0][mine], late[1][mine]], axis=0)
        out_ref[b * BLOCK : (b + 1) * BLOCK, D:] = mm(back, y).astype(bf16)


def against(a, b):
    return lax.dot_general(a, b, (((1,), (1,)), ((), ())), preferred_element_type=f32)


def terms_kernel(
    rows_ref,
    grad_ref,
    bal_ref,
    order_ref,
    place_ref,
    late_ref,
    weight_ref,
    other_ref,
    factor_ref,
):
    cotangent = grad_ref[...]
    scores = against(rows_ref[:, :D], cotangent) * place_ref[...].astype(f32)
    late = against(rows_ref[:, D:], halves(cotangent)) * late_ref[...].astype(f32)
    scores = scores + late[:, :TOK_DEV] + late[:, TOK_DEV:]
    score = jnp.sum(scores.reshape(WIN, WHOLE, TOK_DEV), axis=1)
    weight = weight_ref[...]
    total = jnp.sum(weight[:WIN] * score, axis=0, keepdims=True)
    grad = jnp.concatenate(
        [weight[:WIN] * (score - total), weight[WIN:] * (0.0 - total)], axis=0
    )
    high, low = split2(grad)
    factor = jnp.concatenate(
        [mm(order_ref[...], high).astype(bf16), mm(order_ref[...], low).astype(bf16)], axis=1
    )
    factor_ref[...] = factor[:EXPERTS]
    for half in range(2):
        other_ref[half * EXPERTS : (half + 1) * EXPERTS, :] = half_terms(
            factor[EXPERTS:], bal_ref, half
        ).astype(bf16)


def half_terms(factor, bal_ref, half):
    tokens = bal_ref[:, half * HALF : (half + 1) * HALF]
    term = mm(factor, jnp.concatenate([tokens, tokens], axis=0))
    first = (iota((EXPERTS, QUARTER), 0) & 4) == 0
    return jnp.where(first, term[:, :QUARTER], term[:, QUARTER:])


def join_kernel(factor_ref, bal_ref, given_ref, out_ref):
    for half in range(2):
        rows = slice(half * EXPERTS, (half + 1) * EXPERTS)
        own = half_terms(factor_ref[...], bal_ref, half)
        out_ref[rows, :] = (own + given_ref[rows, :].astype(f32)).astype(bf16)


def output_kernel(
    rows_ref,
    high_ref,
    low_ref,
    late_high_ref,
    late_low_ref,
    factor_ref,
    out_ref,
    handed_ref,
):
    handed_ref[...] = factor_ref[...]
    rows, ends = rows_ref[:, :D], rows_ref[:, D:]
    late = mm(late_high_ref[...], ends) + mm(late_low_ref[...], ends)
    both = mm(high_ref[...], rows) + mm(low_ref[...], rows)
    out_ref[:, :HALF] = (both[:, :HALF] + late[:TOK_DEV]).astype(bf16)
    out_ref[:, HALF:] = (both[:, HALF:] + late[TOK_DEV:]).astype(bf16)


def part_kernel(terms_ref, out_ref):
    part = jnp.sum(terms_ref[...].astype(f32).reshape(2 * CHIPS, 8, QUARTER), axis=0)
    two = jnp.concatenate([part, part], axis=0).astype(bf16)
    for i in range(12):
        out_ref[16 * i : 16 * (i + 1), :] = two


def last_kernel(parts_ref, out_ref):
    parts = jnp.sum(parts_ref[...].astype(f32).reshape(2, 12, 8, QUARTER), axis=1)
    for half in range(2):
        for quarter in range(2):
            at = half * HALF + quarter * QUARTER
            out_ref[:, at : at + QUARTER] = parts[half, 4 * quarter : 4 * quarter + 4]


def in_hbm(array):
    return pltpu.with_memory_space_constraint(array, pltpu.HBM)


def shape(dims, dtype):
    return jax.ShapeDtypeStruct(dims, dtype)


def exchange(blocks, axes, peers):
    rows, cols = blocks.shape
    apart = blocks.reshape(peers, rows // peers, cols)
    return lax.all_to_all(apart, axes, split_axis=0, concat_axis=0, tiled=True).reshape(rows, cols)


def borders(rank, core, flows, rollout, ids, logits):
    return call(
        border_kernel,
        [
            shape((MOVE, D), bf16),
            shape((MOVE, D), bf16),
            shape((SRC_DEV, D), bf16),
            shape((TOK_DEV, SPAN), bf16),
            shape((2 * EXPERTS, EXPERTS), bf16),
            shape((ROWS, TOK_DEV), bf16),
            shape((ROWS, 2 * TOK_DEV), bf16),
            shape((EXPERTS, TOK_DEV), f32),
            shape((TOK_DEV, ROWS), bf16),
            shape((TOK_DEV, ROWS), bf16),
            shape((2 * TOK_DEV, ROWS), bf16),
            shape((2 * TOK_DEV, ROWS), bf16),
        ],
        [SMEM] * 2 + [HBM] * 4,
        25_000_000,
        [
            pltpu.SMEM((1, 24), i32),
            pltpu.VMEM((TOPK, TOK_DEV), i32),
            pltpu.VMEM((TOPK, TOK_DEV), f32),
            pltpu.SemaphoreType.DMA((4,)),
        ],
    )(rank, core, *[in_hbm(v) for v in (flows, rollout, ids, logits)])


def dispatch(left, right, held, settle, place, late):
    return call(
        dispatch_kernel,
        [shape((ROWS, WIDTH), bf16), shape((TOK_DEV, D), bf16)],
        [VMEM] * 6,
        12_000_000_000,
    )(left, right, held, settle, place, late)


def ffn(rows, w_gate, w_up, w_down):
    return call(
        ffn_kernel,
        shape((ROWS, WIDTH), bf16),
        [VMEM] * 4,
        3_700_000_000,
        [pltpu.VMEM((SLOTS, D), bf16), pltpu.VMEM((SLOTS, FF), bf16)],
    )(rows, w_gate, w_up, w_down)


def router_terms(rows, grad_out, balanced, order, place, late, weight):
    return call(
        terms_kernel,
        [shape((2 * EXPERTS, QUARTER), bf16), shape((EXPERTS, 2 * TOK_DEV), bf16)],
        [VMEM] * 7,
        500_000_000,
    )(rows, grad_out, balanced, order, place, late, weight)


def join(factor, balanced, given):
    return call(join_kernel, shape((2 * EXPERTS, QUARTER), bf16), [VMEM] * 3, 150_000_000)(
        factor, balanced, given
    )


def layer_output(rows, shares, factor):
    return call(
        output_kernel,
        [shape((TOK_DEV, D), bf16), shape((EXPERTS, 2 * TOK_DEV), bf16)],
        [VMEM] * 6,
        4_000_000_000,
    )(rows, *shares, factor)


def partial_sum(terms):
    return call(part_kernel, shape((192, QUARTER), bf16), [VMEM], 1_000_000)(terms)


def last_sum(parts):
    return call(last_kernel, shape((4, D), f32), [VMEM], 1_000_000)(parts)


def shards(rollout, flows, route_ids, route_logits, grad_out, w_gate, w_up, w_down):
    ranks = lax.axis_size(DP)
    rank = lax.axis_index(DP).reshape(1)
    core = lax.axis_index("core").reshape(1)
    flows = flows.T
    head, tail, held, settle, order, place, late, weight, *shares = borders(
        rank, core, flows, rollout, route_ids.T, route_logits.T
    )
    left = lax.ppermute(tail, DP, [(i, (i + 1) % ranks) for i in range(ranks)])
    right = lax.ppermute(head, DP, [((i + 1) % ranks, i) for i in range(ranks)])
    outgoing, balanced = dispatch(left, right, held, settle, place, late)
    rows = exchange(outgoing, FSDP, WIN)
    computed = ffn(rows, w_gate, w_up, w_down)
    returned = exchange(computed, FSDP, WIN)
    other, factor = router_terms(returned, grad_out, balanced, order, place, late, weight)
    given = lax.ppermute(other, "core", [(0, 1), (1, 0)])
    layer_out, factor = layer_output(returned, shares, factor)
    terms = exchange(join(factor, balanced, given), ("yl", "chip"), 2 * CHIPS)
    parts = exchange(partial_sum(terms), DP, 24)
    return (layer_out, last_sum(parts))


def solution(mesh):
    fine = Mesh(mesh.devices.reshape(2, 12, CHIPS, 2), DP + FSDP)
    rows = P(DP + FSDP, None)
    expert = P(FSDP, None, None)
    return jax.shard_map(
        shards,
        mesh=fine,
        in_specs=(rows, P(None, FSDP), rows, rows, rows, expert, expert, expert),
        out_specs=(rows, P(FSDP, None)),
        check_vma=False,
    )
```

```python
import jax
import jax.numpy as jnp
from jax import lax
from jax.experimental import pallas as pl
from jax.experimental.pallas import tpu as pltpu
from jax.sharding import Mesh
from jax.sharding import PartitionSpec as P

D = 2048
HALF = D // 2
QUARTER = D // 4
FF = 768
EXPERTS = 128
WIN = 32
TOPK = 8
TOK_DEV = 128
SRC_DEV = 192
MOVE = 32
CAP = 12
SPAN = SRC_DEV + 2 * MOVE
WHOLE = 8
ROWS = WIN * WHOLE
WIDTH = D + HALF
SLOTS = WIN * CAP
BLOCK = 128
DP = ("yl", "z")
FSDP = ("chip", "core")
CHIPS = 16
FF_CHUNK = 256
bf16, f32, i32 = jnp.bfloat16, jnp.float32, jnp.int32
VMEM = pl.BlockSpec(memory_space=pltpu.VMEM)
SMEM = pl.BlockSpec(memory_space=pltpu.SMEM)
HBM = pl.BlockSpec(memory_space=pltpu.HBM)


def iota(shape, dim):
    return lax.broadcasted_iota(i32, shape, dim)


def mm(a, b):
    return jnp.dot(a, b, preferred_element_type=f32)


def split2(v):
    high = v.astype(bf16)
    return high, (v - high.astype(f32)).astype(bf16)


def call(kernel, outs, in_specs, flops, scratch=(), limit=24 << 20):
    many = isinstance(outs, list)
    nbytes = sum(o.size * o.dtype.itemsize for o in (outs if many else [outs]))
    return pl.pallas_call(
        kernel,
        out_shape=outs,
        in_specs=in_specs,
        out_specs=[VMEM] * len(outs) if many else VMEM,
        scratch_shapes=list(scratch),
        cost_estimate=pl.CostEstimate(
            flops=flops, bytes_accessed=2 * nbytes, transcendentals=0
        ),
        compiler_params=pltpu.CompilerParams(vmem_limit_bytes=limit),
    )


def border_kernel(
    rank_ref,
    core_ref,
    flows_hbm,
    rollout_hbm,
    ids_hbm,
    logits_hbm,
    head_ref,
    tail_ref,
    held_ref,
    settle_ref,
    order_ref,
    place_ref,
    late_ref,
    weight_ref,
    high_ref,
    low_ref,
    late_high_ref,
    late_low_ref,
    flows,
    ids,
    logits,
    sems,
):
    flow_copy = pltpu.make_async_copy(flows_hbm, flows, sems.at[0])
    ids_copy = pltpu.make_async_copy(ids_hbm, ids, sems.at[1])
    logits_copy = pltpu.make_async_copy(logits_hbm, logits, sems.at[2])
    held_copy = pltpu.make_async_copy(rollout_hbm, held_ref, sems.at[3])
    flow_copy.start()
    ids_copy.start()
    logits_copy.start()
    held_copy.start()
    ids_copy.wait()
    logits_copy.wait()
    route(
        ids,
        logits[...],
        place_ref,
        late_ref,
        weight_ref,
        (high_ref, low_ref),
        (late_high_ref, late_low_ref),
    )
    line = iota((2 * EXPERTS, EXPERTS), 0)
    core = jnp.where(line < EXPERTS, core_ref[0], 1 - core_ref[0])
    expert = ((line >> 3) & 15) * 8 + 4 * core + (line & 3)
    order_ref[...] = (iota((2 * EXPERTS, EXPERTS), 1) == expert).astype(bf16)
    flow_copy.wait()
    rank = rank_ref[0]
    left = flows[0, jnp.where(rank == 0, 23, rank - 1)]
    live = TOK_DEV + flows[0, rank] - left
    at = iota((TOK_DEV, SPAN), 0) + (MOVE - left)
    at = jnp.where(at < MOVE + live, at, at + (SRC_DEV - live))
    settle_ref[...] = (iota((TOK_DEV, SPAN), 1) == at).astype(bf16)
    at = iota((MOVE, SRC_DEV), 0) + (live - MOVE)
    pick = (iota((MOVE, SRC_DEV), 1) == at).astype(bf16)
    held_copy.wait()
    head_ref[...] = held_ref[:MOVE, :]
    tail_ref[...] = mm(pick, held_ref[...]).astype(bf16)


def route(ids, logits, place_ref, late_ref, weight_ref, parts_refs, late_parts_refs):
    raised = jnp.exp(logits - jnp.max(logits, axis=0, keepdims=True))
    share = raised / jnp.sum(raised, axis=0, keepdims=True)
    expert = iota((EXPERTS, TOK_DEV), 0)
    weight = jnp.zeros((EXPERTS, TOK_DEV), f32)
    named = jnp.zeros((EXPERTS, TOK_DEV), f32)
    for k in range(TOPK):
        hit = ids[k : k + 1, :] == expert
        weight = jnp.where(hit, share[k : k + 1, :], weight)
        named = jnp.where(hit, 1.0, named)
    weight_ref[...] = weight
    upto = (iota((TOK_DEV, TOK_DEV), 0) <= iota((TOK_DEV, TOK_DEV), 1)).astype(bf16)
    count = mm(named[:WIN].astype(bf16), upto)
    code = jnp.where(named[:WIN] > 0.0, count, 0.0).astype(bf16)
    spread = ((iota((ROWS, WIN), 0) >> 3) == iota((ROWS, WIN), 1)).astype(bf16)
    row = iota((ROWS, TOK_DEV), 0)
    codes = mm(spread, code).astype(i32)
    whole = codes == (row & 7) + 1
    late = codes == (row & 3) + (WHOLE + 1)
    second = (row & 4) == 4
    place_ref[...] = whole.astype(bf16)
    for half in range(2):
        cols = slice(half * TOK_DEV, (half + 1) * TOK_DEV)
        late_ref[:, cols] = (late & (second == (half == 1))).astype(bf16)
    for part, out, late_out in zip(split2(weight[:WIN]), parts_refs, late_parts_refs):
        spreads = mm(spread, part)
        out[...] = jnp.where(whole, spreads, 0.0).T.astype(bf16)
        for half in range(2):
            mine = late & (second == (half == 1))
            late_out[half * TOK_DEV : (half + 1) * TOK_DEV, :] = (
                jnp.where(mine, spreads, 0.0).T.astype(bf16)
            )


def halves(wide):
    return jnp.concatenate([wide[:, :HALF], wide[:, HALF:]], axis=0)


def dispatch_kernel(
    left_ref, right_ref, held_ref, settle_ref, place_ref, late_ref, out_ref, bal_ref
):
    rows = jnp.concatenate([left_ref[...], held_ref[...], right_ref[...]], axis=0)
    balanced = mm(settle_ref[...], rows).astype(bf16)
    bal_ref[...] = balanced
    out_ref[:, :D] = mm(place_ref[...], balanced).astype(bf16)
    out_ref[:, D:] = mm(late_ref[...], halves(balanced)).astype(bf16)


def block_source(dim):
    row = iota((BLOCK, BLOCK), dim)
    return ((row >> 2) & 15) * 8 + (row >> 6) * 4 + (row & 3)


def ffn_kernel(rows_ref, gate_ref, up_ref, down_ref, out_ref, x, hidden):
    ordered = (iota((BLOCK, BLOCK), 1) == block_source(0)).astype(bf16)
    back = (iota((BLOCK, BLOCK), 0) == block_source(1)).astype(bf16)
    part_rows = BLOCK // 2
    x[:ROWS, :] = rows_ref[:, :D]
    for b in range(ROWS // BLOCK):
        y = mm(ordered, rows_ref[b * BLOCK : (b + 1) * BLOCK, D:]).astype(bf16)
        mine = slice(ROWS + b * part_rows, ROWS + (b + 1) * part_rows)
        x[mine, :HALF] = y[:part_rows]
        x[mine, HALF:] = y[part_rows:]
    for f in range(FF // FF_CHUNK):
        cols = slice(f * FF_CHUNK, (f + 1) * FF_CHUNK)
        g = mm(x[...], gate_ref[0, :, cols])
        u = mm(x[...], up_ref[0, :, cols])
        hidden[:, cols] = (g / (1.0 + jnp.exp(-g)) * u).astype(bf16)
    late = []
    for half in range(2):
        cols = slice(half * HALF, (half + 1) * HALF)
        y = mm(hidden[...], down_ref[0, :, cols]).astype(bf16)
        out_ref[:, cols] = y[:ROWS]
        late.append(y[ROWS:])
    for b in range(ROWS // BLOCK):
        mine = slice(b * part_rows, (b + 1) * part_rows)
        y = jnp.concatenate([late[0][mine], late[1][mine]], axis=0)
        out_ref[b * BLOCK : (b + 1) * BLOCK, D:] = mm(back, y).astype(bf16)


def against(a, b):
    return lax.dot_general(a, b, (((1,), (1,)), ((), ())), preferred_element_type=f32)


def terms_kernel(
    rows_ref,
    grad_ref,
    bal_ref,
    order_ref,
    place_ref,
    late_ref,
    weight_ref,
    other_ref,
    factor_ref,
):
    cotangent = grad_ref[...]
    scores = against(rows_ref[:, :D], cotangent) * place_ref[...].astype(f32)
    late = against(rows_ref[:, D:], halves(cotangent)) * late_ref[...].astype(f32)
    scores = scores + late[:, :TOK_DEV] + late[:, TOK_DEV:]
    score = jnp.sum(scores.reshape(WIN, WHOLE, TOK_DEV), axis=1)
    weight = weight_ref[...]
    total = jnp.sum(weight[:WIN] * score, axis=0, keepdims=True)
    grad = jnp.concatenate(
        [weight[:WIN] * (score - total), weight[WIN:] * (0.0 - total)], axis=0
    )
    high, low = split2(grad)
    factor = jnp.concatenate(
        [mm(order_ref[...], high).astype(bf16), mm(order_ref[...], low).astype(bf16)], axis=1
    )
    factor_ref[...] = factor[:EXPERTS]
    for half in range(2):
        other_ref[half * EXPERTS : (half + 1) * EXPERTS, :] = half_terms(
            factor[EXPERTS:], bal_ref, half
        ).astype(bf16)


def half_terms(factor, bal_ref, half):
    tokens = bal_ref[:, half * HALF : (half + 1) * HALF]
    term = mm(factor, jnp.concatenate([tokens, tokens], axis=0))
    first = (iota((EXPERTS, QUARTER), 0) & 4) == 0
    return jnp.where(first, term[:, :QUARTER], term[:, QUARTER:])


def join_kernel(factor_ref, bal_ref, given_ref, out_ref):
    for half in range(2):
        rows = slice(half * EXPERTS, (half + 1) * EXPERTS)
        own = half_terms(factor_ref[...], bal_ref, half)
        out_ref[rows, :] = (own + given_ref[rows, :].astype(f32)).astype(bf16)


def output_kernel(
    rows_ref,
    high_ref,
    low_ref,
    late_high_ref,
    late_low_ref,
    factor_ref,
    out_ref,
    handed_ref,
):
    handed_ref[...] = factor_ref[...]
    rows, ends = rows_ref[:, :D], rows_ref[:, D:]
    late = mm(late_high_ref[...], ends) + mm(late_low_ref[...], ends)
    both = mm(high_ref[...], rows) + mm(low_ref[...], rows)
    out_ref[:, :HALF] = (both[:, :HALF] + late[:TOK_DEV]).astype(bf16)
    out_ref[:, HALF:] = (both[:, HALF:] + late[TOK_DEV:]).astype(bf16)


def part_kernel(terms_ref, out_ref):
    part = jnp.sum(terms_ref[...].astype(f32).reshape(2 * CHIPS, 8, QUARTER), axis=0)
    two = jnp.concatenate([part, part], axis=0).astype(bf16)
    for i in range(12):
        out_ref[16 * i : 16 * (i + 1), :] = two


def last_kernel(parts_ref, out_ref):
    parts = jnp.sum(parts_ref[...].astype(f32).reshape(2, 12, 8, QUARTER), axis=1)
    for half in range(2):
        for quarter in range(2):
            at = half * HALF + quarter * QUARTER
            out_ref[:, at : at + QUARTER] = parts[half, 4 * quarter : 4 * quarter + 4]


def in_hbm(array):
    return pltpu.with_memory_space_constraint(array, pltpu.HBM)


def shape(dims, dtype):
    return jax.ShapeDtypeStruct(dims, dtype)


def exchange(blocks, axes, peers, groups=None):
    rows, cols = blocks.shape
    apart = blocks.reshape(peers, rows // peers, cols)
    return lax.all_to_all(
        apart, axes, split_axis=0, concat_axis=0, axis_index_groups=groups, tiled=True
    ).reshape(rows, cols)


def expert_groups():
    return [
        [
            (((side ^ (chip >= CHIPS // 2)) * 12 + z) * CHIPS + chip) * 2 + core
            for chip in range(CHIPS)
            for core in range(2)
        ]
        for z in range(12)
        for side in range(2)
    ]


def borders(rank, core, flows, rollout, ids, logits):
    return call(
        border_kernel,
        [
            shape((MOVE, D), bf16),
            shape((MOVE, D), bf16),
            shape((SRC_DEV, D), bf16),
            shape((TOK_DEV, SPAN), bf16),
            shape((2 * EXPERTS, EXPERTS), bf16),
            shape((ROWS, TOK_DEV), bf16),
            shape((ROWS, 2 * TOK_DEV), bf16),
            shape((EXPERTS, TOK_DEV), f32),
            shape((TOK_DEV, ROWS), bf16),
            shape((TOK_DEV, ROWS), bf16),
            shape((2 * TOK_DEV, ROWS), bf16),
            shape((2 * TOK_DEV, ROWS), bf16),
        ],
        [SMEM] * 2 + [HBM] * 4,
        25_000_000,
        [
            pltpu.SMEM((1, 24), i32),
            pltpu.VMEM((TOPK, TOK_DEV), i32),
            pltpu.VMEM((TOPK, TOK_DEV), f32),
            pltpu.SemaphoreType.DMA((4,)),
        ],
    )(rank, core, *[in_hbm(v) for v in (flows, rollout, ids, logits)])


def dispatch(left, right, held, settle, place, late):
    return call(
        dispatch_kernel,
        [shape((ROWS, WIDTH), bf16), shape((TOK_DEV, D), bf16)],
        [VMEM] * 6,
        12_000_000_000,
    )(left, right, held, settle, place, late)


def ffn(rows, w_gate, w_up, w_down):
    return call(
        ffn_kernel,
        shape((ROWS, WIDTH), bf16),
        [VMEM] * 4,
        3_700_000_000,
        [pltpu.VMEM((SLOTS, D), bf16), pltpu.VMEM((SLOTS, FF), bf16)],
    )(rows, w_gate, w_up, w_down)


def router_terms(rows, grad_out, balanced, order, place, late, weight):
    return call(
        terms_kernel,
        [shape((2 * EXPERTS, QUARTER), bf16), shape((EXPERTS, 2 * TOK_DEV), bf16)],
        [VMEM] * 7,
        500_000_000,
    )(rows, grad_out, balanced, order, place, late, weight)


def join(factor, balanced, given):
    return call(join_kernel, shape((2 * EXPERTS, QUARTER), bf16), [VMEM] * 3, 150_000_000)(
        factor, balanced, given
    )


def layer_output(rows, shares, factor):
    return call(
        output_kernel,
        [shape((TOK_DEV, D), bf16), shape((EXPERTS, 2 * TOK_DEV), bf16)],
        [VMEM] * 6,
        4_000_000_000,
    )(rows, *shares, factor)


def partial_sum(terms):
    return call(part_kernel, shape((192, QUARTER), bf16), [VMEM], 1_000_000)(terms)


def last_sum(parts):
    return call(last_kernel, shape((4, D), f32), [VMEM], 1_000_000)(parts)


def shards(rollout, flows, route_ids, route_logits, grad_out, w_gate, w_up, w_down):
    ranks = lax.axis_size(DP)
    rank = lax.axis_index(DP).reshape(1)
    core = lax.axis_index("core").reshape(1)
    flows = flows.T
    head, tail, held, settle, order, place, late, weight, *shares = borders(
        rank, core, flows, rollout, route_ids.T, route_logits.T
    )
    left = lax.ppermute(tail, DP, [(i, (i + 1) % ranks) for i in range(ranks)])
    right = lax.ppermute(head, DP, [((i + 1) % ranks, i) for i in range(ranks)])
    outgoing, balanced = dispatch(left, right, held, settle, place, late)
    rows = exchange(outgoing, DP + FSDP, WIN, expert_groups())
    computed = ffn(rows, w_gate, w_up, w_down)
    returned = exchange(computed, DP + FSDP, WIN, expert_groups())
    other, factor = router_terms(returned, grad_out, balanced, order, place, late, weight)
    given = lax.ppermute(other, "core", [(0, 1), (1, 0)])
    layer_out, factor = layer_output(returned, shares, factor)
    terms = exchange(join(factor, balanced, given), ("yl", "chip"), 2 * CHIPS)
    parts = exchange(partial_sum(terms), DP, 24)
    return (layer_out, last_sum(parts))


def solution(mesh):
    fine = Mesh(mesh.devices.reshape(2, 12, CHIPS, 2), DP + FSDP)
    rows = P(DP + FSDP, None)
    expert = P(FSDP, None, None)
    return jax.shard_map(
        shards,
        mesh=fine,
        in_specs=(rows, P(None, FSDP), rows, rows, rows, expert, expert, expert),
        out_specs=(rows, P(FSDP, None)),
        check_vma=False,
    )
```

```python
import jax
import jax.numpy as jnp
from jax import lax
from jax.experimental import pallas as pl
from jax.experimental.pallas import tpu as pltpu
from jax.sharding import Mesh
from jax.sharding import PartitionSpec as P

D = 2048
HALF = D // 2
QUARTER = D // 4
FF = 768
EXPERTS = 128
WIN = 32
TOPK = 8
TOK_DEV = 128
SRC_DEV = 192
MOVE = 32
CAP = 12
SPAN = SRC_DEV + 2 * MOVE
WHOLE = 8
ROWS = WIN * WHOLE
WIDTH = D + HALF
SLOTS = WIN * CAP
BLOCK = 128
DP = ("yl", "z")
FSDP = ("chip", "core")
CHIPS = 16
FF_CHUNK = 256
bf16, f32, i32 = jnp.bfloat16, jnp.float32, jnp.int32
VMEM = pl.BlockSpec(memory_space=pltpu.VMEM)
SMEM = pl.BlockSpec(memory_space=pltpu.SMEM)
HBM = pl.BlockSpec(memory_space=pltpu.HBM)


def iota(shape, dim):
    return lax.broadcasted_iota(i32, shape, dim)


def mm(a, b):
    return jnp.dot(a, b, preferred_element_type=f32)


def split2(v):
    high = v.astype(bf16)
    return high, (v - high.astype(f32)).astype(bf16)


def call(kernel, outs, in_specs, flops, scratch=(), limit=24 << 20):
    many = isinstance(outs, list)
    nbytes = sum(o.size * o.dtype.itemsize for o in (outs if many else [outs]))
    return pl.pallas_call(
        kernel,
        out_shape=outs,
        in_specs=in_specs,
        out_specs=[VMEM] * len(outs) if many else VMEM,
        scratch_shapes=list(scratch),
        cost_estimate=pl.CostEstimate(
            flops=flops, bytes_accessed=2 * nbytes, transcendentals=0
        ),
        compiler_params=pltpu.CompilerParams(vmem_limit_bytes=limit),
    )


def border_kernel(
    rank_ref,
    core_ref,
    flows_hbm,
    rollout_hbm,
    ids_hbm,
    logits_hbm,
    tail_ref,
    held_ref,
    settle_ref,
    order_ref,
    place_ref,
    late_ref,
    weight_ref,
    high_ref,
    low_ref,
    late_high_ref,
    late_low_ref,
    flows,
    ids,
    logits,
    sems,
):
    flow_copy = pltpu.make_async_copy(flows_hbm, flows, sems.at[0])
    ids_copy = pltpu.make_async_copy(ids_hbm, ids, sems.at[1])
    logits_copy = pltpu.make_async_copy(logits_hbm, logits, sems.at[2])
    held_copy = pltpu.make_async_copy(rollout_hbm, held_ref, sems.at[3])
    flow_copy.start()
    ids_copy.start()
    logits_copy.start()
    held_copy.start()
    ids_copy.wait()
    logits_copy.wait()
    route(
        ids,
        logits[...],
        place_ref,
        late_ref,
        weight_ref,
        (high_ref, low_ref),
        (late_high_ref, late_low_ref),
    )
    line = iota((2 * EXPERTS, EXPERTS), 0)
    core = jnp.where(line < EXPERTS, core_ref[0], 1 - core_ref[0])
    expert = ((line >> 3) & 15) * 8 + 4 * core + (line & 3)
    order_ref[...] = (iota((2 * EXPERTS, EXPERTS), 1) == expert).astype(bf16)
    flow_copy.wait()
    rank = rank_ref[0]
    left = flows[0, jnp.where(rank == 0, 23, rank - 1)]
    live = TOK_DEV + flows[0, rank] - left
    at = iota((TOK_DEV, SPAN), 0) + (MOVE - left)
    at = jnp.where(at < MOVE + live, at, at + (SRC_DEV - live))
    settle_ref[...] = (iota((TOK_DEV, SPAN), 1) == at).astype(bf16)
    at = iota((MOVE, SRC_DEV), 0) + (live - MOVE)
    pick = (iota((MOVE, SRC_DEV), 1) == at).astype(bf16)
    held_copy.wait()
    tail_ref[...] = mm(pick, held_ref[...]).astype(bf16)


def route(ids, logits, place_ref, late_ref, weight_ref, parts_refs, late_parts_refs):
    raised = jnp.exp(logits - jnp.max(logits, axis=0, keepdims=True))
    share = raised / jnp.sum(raised, axis=0, keepdims=True)
    expert = iota((EXPERTS, TOK_DEV), 0)
    weight = jnp.zeros((EXPERTS, TOK_DEV), f32)
    named = jnp.zeros((EXPERTS, TOK_DEV), f32)
    for k in range(TOPK):
        hit = ids[k : k + 1, :] == expert
        weight = jnp.where(hit, share[k : k + 1, :], weight)
        named = jnp.where(hit, 1.0, named)
    weight_ref[...] = weight
    upto = (iota((TOK_DEV, TOK_DEV), 0) <= iota((TOK_DEV, TOK_DEV), 1)).astype(bf16)
    count = mm(named[:WIN].astype(bf16), upto)
    code = jnp.where(named[:WIN] > 0.0, count, 0.0).astype(bf16)
    spread = ((iota((ROWS, WIN), 0) >> 3) == iota((ROWS, WIN), 1)).astype(bf16)
    row = iota((ROWS, TOK_DEV), 0)
    codes = mm(spread, code).astype(i32)
    whole = codes == (row & 7) + 1
    late = codes == (row & 3) + (WHOLE + 1)
    second = (row & 4) == 4
    place_ref[...] = whole.astype(bf16)
    for half in range(2):
        cols = slice(half * TOK_DEV, (half + 1) * TOK_DEV)
        late_ref[:, cols] = (late & (second == (half == 1))).astype(bf16)
    for part, out, late_out in zip(split2(weight[:WIN]), parts_refs, late_parts_refs):
        spreads = mm(spread, part)
        out[...] = jnp.where(whole, spreads, 0.0).T.astype(bf16)
        for half in range(2):
            mine = late & (second == (half == 1))
            late_out[half * TOK_DEV : (half + 1) * TOK_DEV, :] = (
                jnp.where(mine, spreads, 0.0).T.astype(bf16)
            )


def halves(wide):
    return jnp.concatenate([wide[:, :HALF], wide[:, HALF:]], axis=0)


def dispatch_kernel(
    left_ref, right_ref, held_ref, settle_ref, place_ref, late_ref, out_ref, bal_ref
):
    rows = jnp.concatenate([left_ref[...], held_ref[...], right_ref[...]], axis=0)
    balanced = mm(settle_ref[...], rows).astype(bf16)
    bal_ref[...] = balanced
    out_ref[:, :D] = mm(place_ref[...], balanced).astype(bf16)
    out_ref[:, D:] = mm(late_ref[...], halves(balanced)).astype(bf16)


def block_source(dim):
    row = iota((BLOCK, BLOCK), dim)
    return ((row >> 2) & 15) * 8 + (row >> 6) * 4 + (row & 3)


def ffn_kernel(rows_ref, gate_ref, up_ref, down_ref, out_ref, x, hidden):
    ordered = (iota((BLOCK, BLOCK), 1) == block_source(0)).astype(bf16)
    back = (iota((BLOCK, BLOCK), 0) == block_source(1)).astype(bf16)
    part_rows = BLOCK // 2
    x[:ROWS, :] = rows_ref[:, :D]
    for b in range(ROWS // BLOCK):
        y = mm(ordered, rows_ref[b * BLOCK : (b + 1) * BLOCK, D:]).astype(bf16)
        mine = slice(ROWS + b * part_rows, ROWS + (b + 1) * part_rows)
        x[mine, :HALF] = y[:part_rows]
        x[mine, HALF:] = y[part_rows:]
    for f in range(FF // FF_CHUNK):
        cols = slice(f * FF_CHUNK, (f + 1) * FF_CHUNK)
        g = mm(x[...], gate_ref[0, :, cols])
        u = mm(x[...], up_ref[0, :, cols])
        hidden[:, cols] = (g / (1.0 + jnp.exp(-g)) * u).astype(bf16)
    late = []
    for half in range(2):
        cols = slice(half * HALF, (half + 1) * HALF)
        y = mm(hidden[...], down_ref[0, :, cols]).astype(bf16)
        out_ref[:, cols] = y[:ROWS]
        late.append(y[ROWS:])
    for b in range(ROWS // BLOCK):
        mine = slice(b * part_rows, (b + 1) * part_rows)
        y = jnp.concatenate([late[0][mine], late[1][mine]], axis=0)
        out_ref[b * BLOCK : (b + 1) * BLOCK, D:] = mm(back, y).astype(bf16)


def against(a, b):
    return lax.dot_general(a, b, (((1,), (1,)), ((), ())), preferred_element_type=f32)


def terms_kernel(
    rows_ref,
    grad_ref,
    bal_ref,
    order_ref,
    place_ref,
    late_ref,
    weight_ref,
    other_ref,
    factor_ref,
):
    cotangent = grad_ref[...]
    scores = against(rows_ref[:, :D], cotangent) * place_ref[...].astype(f32)
    late = against(rows_ref[:, D:], halves(cotangent)) * late_ref[...].astype(f32)
    scores = scores + late[:, :TOK_DEV] + late[:, TOK_DEV:]
    score = jnp.sum(scores.reshape(WIN, WHOLE, TOK_DEV), axis=1)
    weight = weight_ref[...]
    total = jnp.sum(weight[:WIN] * score, axis=0, keepdims=True)
    grad = jnp.concatenate(
        [weight[:WIN] * (score - total), weight[WIN:] * (0.0 - total)], axis=0
    )
    high, low = split2(grad)
    factor = jnp.concatenate(
        [mm(order_ref[...], high).astype(bf16), mm(order_ref[...], low).astype(bf16)], axis=1
    )
    factor_ref[...] = factor[:EXPERTS]
    for half in range(2):
        other_ref[half * EXPERTS : (half + 1) * EXPERTS, :] = half_terms(
            factor[EXPERTS:], bal_ref, half
        ).astype(bf16)


def half_terms(factor, bal_ref, half):
    tokens = bal_ref[:, half * HALF : (half + 1) * HALF]
    term = mm(factor, jnp.concatenate([tokens, tokens], axis=0))
    first = (iota((EXPERTS, QUARTER), 0) & 4) == 0
    return jnp.where(first, term[:, :QUARTER], term[:, QUARTER:])


def join_kernel(factor_ref, bal_ref, given_ref, out_ref):
    for half in range(2):
        rows = slice(half * EXPERTS, (half + 1) * EXPERTS)
        own = half_terms(factor_ref[...], bal_ref, half)
        out_ref[rows, :] = (own + given_ref[rows, :].astype(f32)).astype(bf16)


def output_kernel(
    rows_ref,
    high_ref,
    low_ref,
    late_high_ref,
    late_low_ref,
    factor_ref,
    out_ref,
    handed_ref,
):
    handed_ref[...] = factor_ref[...]
    rows, ends = rows_ref[:, :D], rows_ref[:, D:]
    late = mm(late_high_ref[...], ends) + mm(late_low_ref[...], ends)
    both = mm(high_ref[...], rows) + mm(low_ref[...], rows)
    out_ref[:, :HALF] = (both[:, :HALF] + late[:TOK_DEV]).astype(bf16)
    out_ref[:, HALF:] = (both[:, HALF:] + late[TOK_DEV:]).astype(bf16)


def part_kernel(terms_ref, out_ref):
    part = jnp.sum(terms_ref[...].astype(f32).reshape(2 * CHIPS, 8, QUARTER), axis=0)
    two = jnp.concatenate([part, part], axis=0).astype(bf16)
    for i in range(12):
        out_ref[16 * i : 16 * (i + 1), :] = two


def last_kernel(parts_ref, out_ref):
    parts = jnp.sum(parts_ref[...].astype(f32).reshape(2, 12, 8, QUARTER), axis=1)
    for half in range(2):
        for quarter in range(2):
            at = half * HALF + quarter * QUARTER
            out_ref[:, at : at + QUARTER] = parts[half, 4 * quarter : 4 * quarter + 4]


def in_hbm(array):
    return pltpu.with_memory_space_constraint(array, pltpu.HBM)


def shape(dims, dtype):
    return jax.ShapeDtypeStruct(dims, dtype)


def exchange(blocks, axes, peers, groups=None):
    rows, cols = blocks.shape
    apart = blocks.reshape(peers, rows // peers, cols)
    return lax.all_to_all(
        apart, axes, split_axis=0, concat_axis=0, axis_index_groups=groups, tiled=True
    ).reshape(rows, cols)


def expert_groups():
    return [
        [
            (((side ^ (chip >= CHIPS // 2)) * 12 + z) * CHIPS + chip) * 2 + core
            for chip in range(CHIPS)
            for core in range(2)
        ]
        for z in range(12)
        for side in range(2)
    ]


def borders(rank, core, flows, rollout, ids, logits):
    return call(
        border_kernel,
        [
            shape((MOVE, D), bf16),
            shape((SRC_DEV, D), bf16),
            shape((TOK_DEV, SPAN), bf16),
            shape((2 * EXPERTS, EXPERTS), bf16),
            shape((ROWS, TOK_DEV), bf16),
            shape((ROWS, 2 * TOK_DEV), bf16),
            shape((EXPERTS, TOK_DEV), f32),
            shape((TOK_DEV, ROWS), bf16),
            shape((TOK_DEV, ROWS), bf16),
            shape((2 * TOK_DEV, ROWS), bf16),
            shape((2 * TOK_DEV, ROWS), bf16),
        ],
        [SMEM] * 2 + [HBM] * 4,
        25_000_000,
        [
            pltpu.SMEM((1, 24), i32),
            pltpu.VMEM((TOPK, TOK_DEV), i32),
            pltpu.VMEM((TOPK, TOK_DEV), f32),
            pltpu.SemaphoreType.DMA((4,)),
        ],
    )(rank, core, *[in_hbm(v) for v in (flows, rollout, ids, logits)])


def dispatch(left, right, held, settle, place, late):
    return call(
        dispatch_kernel,
        [shape((ROWS, WIDTH), bf16), shape((TOK_DEV, D), bf16)],
        [VMEM] * 6,
        12_000_000_000,
    )(left, right, held, settle, place, late)


def ffn(rows, w_gate, w_up, w_down):
    return call(
        ffn_kernel,
        shape((ROWS, WIDTH), bf16),
        [VMEM] * 4,
        3_700_000_000,
        [pltpu.VMEM((SLOTS, D), bf16), pltpu.VMEM((SLOTS, FF), bf16)],
    )(rows, w_gate, w_up, w_down)


def router_terms(rows, grad_out, balanced, order, place, late, weight):
    return call(
        terms_kernel,
        [shape((2 * EXPERTS, QUARTER), bf16), shape((EXPERTS, 2 * TOK_DEV), bf16)],
        [VMEM] * 7,
        500_000_000,
    )(rows, grad_out, balanced, order, place, late, weight)


def join(factor, balanced, given):
    return call(join_kernel, shape((2 * EXPERTS, QUARTER), bf16), [VMEM] * 3, 150_000_000)(
        factor, balanced, given
    )


def layer_output(rows, shares, factor):
    return call(
        output_kernel,
        [shape((TOK_DEV, D), bf16), shape((EXPERTS, 2 * TOK_DEV), bf16)],
        [VMEM] * 6,
        4_000_000_000,
    )(rows, *shares, factor)


def partial_sum(terms):
    return call(part_kernel, shape((192, QUARTER), bf16), [VMEM], 1_000_000)(terms)


def last_sum(parts):
    return call(last_kernel, shape((4, D), f32), [VMEM], 1_000_000)(parts)


def shards(rollout, flows, route_ids, route_logits, grad_out, w_gate, w_up, w_down):
    ranks = lax.axis_size(DP)
    rank = lax.axis_index(DP).reshape(1)
    core = lax.axis_index("core").reshape(1)
    flows = flows.T
    right = lax.ppermute(rollout[:MOVE], DP, [((i + 1) % ranks, i) for i in range(ranks)])
    tail, held, settle, order, place, late, weight, *shares = borders(
        rank, core, flows, rollout, route_ids.T, route_logits.T
    )
    left = lax.ppermute(tail, DP, [(i, (i + 1) % ranks) for i in range(ranks)])
    outgoing, balanced = dispatch(left, right, held, settle, place, late)
    rows = exchange(outgoing, DP + FSDP, WIN, expert_groups())
    computed = ffn(rows, w_gate, w_up, w_down)
    returned = exchange(computed, DP + FSDP, WIN, expert_groups())
    other, factor = router_terms(returned, grad_out, balanced, order, place, late, weight)
    given = lax.ppermute(other, "core", [(0, 1), (1, 0)])
    layer_out, factor = layer_output(returned, shares, factor)
    terms = exchange(join(factor, balanced, given), ("yl", "chip"), 2 * CHIPS)
    parts = exchange(partial_sum(terms), DP, 24)
    return (layer_out, last_sum(parts))


def solution(mesh):
    fine = Mesh(mesh.devices.reshape(2, 12, CHIPS, 2), DP + FSDP)
    rows = P(DP + FSDP, None)
    expert = P(FSDP, None, None)
    return jax.shard_map(
        shards,
        mesh=fine,
        in_specs=(rows, P(None, FSDP), rows, rows, rows, expert, expert, expert),
        out_specs=(rows, P(FSDP, None)),
        check_vma=False,
    )
```

```python
import jax
import jax.numpy as jnp
from jax import lax
from jax.experimental import pallas as pl
from jax.experimental.pallas import tpu as pltpu
from jax.sharding import Mesh
from jax.sharding import PartitionSpec as P

D = 2048
HALF = D // 2
QUARTER = D // 4
FF = 768
EXPERTS = 128
WIN = 32
TOPK = 8
TOK_DEV = 128
SRC_DEV = 192
MOVE = 32
CAP = 12
SPAN = SRC_DEV + 2 * MOVE
WHOLE = 8
ROWS = WIN * WHOLE
WIDTH = D + HALF
SLOTS = WIN * CAP
BLOCK = 128
DP = ("yl", "z")
FSDP = ("chip", "core")
CHIPS = 16
FF_CHUNK = 768
bf16, f32, i32 = jnp.bfloat16, jnp.float32, jnp.int32
VMEM = pl.BlockSpec(memory_space=pltpu.VMEM)
SMEM = pl.BlockSpec(memory_space=pltpu.SMEM)
HBM = pl.BlockSpec(memory_space=pltpu.HBM)


def iota(shape, dim):
    return lax.broadcasted_iota(i32, shape, dim)


def mm(a, b):
    return jnp.dot(a, b, preferred_element_type=f32)


def split2(v):
    high = v.astype(bf16)
    return high, (v - high.astype(f32)).astype(bf16)


def call(kernel, outs, in_specs, flops, scratch=(), limit=24 << 20):
    many = isinstance(outs, list)
    nbytes = sum(o.size * o.dtype.itemsize for o in (outs if many else [outs]))
    return pl.pallas_call(
        kernel,
        out_shape=outs,
        in_specs=in_specs,
        out_specs=[VMEM] * len(outs) if many else VMEM,
        scratch_shapes=list(scratch),
        cost_estimate=pl.CostEstimate(
            flops=flops, bytes_accessed=2 * nbytes, transcendentals=0
        ),
        compiler_params=pltpu.CompilerParams(vmem_limit_bytes=limit),
    )


def border_kernel(
    rank_ref,
    core_ref,
    flows_hbm,
    rollout_hbm,
    ids_hbm,
    logits_hbm,
    head_ref,
    tail_ref,
    held_ref,
    settle_ref,
    order_ref,
    place_ref,
    late_ref,
    weight_ref,
    high_ref,
    low_ref,
    late_high_ref,
    late_low_ref,
    flows,
    ids,
    logits,
    sems,
):
    flow_copy = pltpu.make_async_copy(flows_hbm, flows, sems.at[0])
    ids_copy = pltpu.make_async_copy(ids_hbm, ids, sems.at[1])
    logits_copy = pltpu.make_async_copy(logits_hbm, logits, sems.at[2])
    held_copy = pltpu.make_async_copy(rollout_hbm, held_ref, sems.at[3])
    flow_copy.start()
    ids_copy.start()
    logits_copy.start()
    held_copy.start()
    ids_copy.wait()
    logits_copy.wait()
    route(
        ids,
        logits[...],
        place_ref,
        late_ref,
        weight_ref,
        (high_ref, low_ref),
        (late_high_ref, late_low_ref),
    )
    line = iota((2 * EXPERTS, EXPERTS), 0)
    core = jnp.where(line < EXPERTS, core_ref[0], 1 - core_ref[0])
    expert = ((line >> 3) & 15) * 8 + 4 * core + (line & 3)
    order_ref[...] = (iota((2 * EXPERTS, EXPERTS), 1) == expert).astype(bf16)
    flow_copy.wait()
    rank = rank_ref[0]
    left = flows[0, jnp.where(rank == 0, 23, rank - 1)]
    live = TOK_DEV + flows[0, rank] - left
    at = iota((TOK_DEV, SPAN), 0) + (MOVE - left)
    at = jnp.where(at < MOVE + live, at, at + (SRC_DEV - live))
    settle_ref[...] = (iota((TOK_DEV, SPAN), 1) == at).astype(bf16)
    at = iota((MOVE, SRC_DEV), 0) + (live - MOVE)
    pick = (iota((MOVE, SRC_DEV), 1) == at).astype(bf16)
    held_copy.wait()
    head_ref[...] = held_ref[:MOVE, :]
    tail_ref[...] = mm(pick, held_ref[...]).astype(bf16)


def route(ids, logits, place_ref, late_ref, weight_ref, parts_refs, late_parts_refs):
    raised = jnp.exp(logits - jnp.max(logits, axis=0, keepdims=True))
    share = raised / jnp.sum(raised, axis=0, keepdims=True)
    expert = iota((EXPERTS, TOK_DEV), 0)
    weight = jnp.zeros((EXPERTS, TOK_DEV), f32)
    named = jnp.zeros((EXPERTS, TOK_DEV), f32)
    for k in range(TOPK):
        hit = ids[k : k + 1, :] == expert
        weight = jnp.where(hit, share[k : k + 1, :], weight)
        named = jnp.where(hit, 1.0, named)
    weight_ref[...] = weight
    upto = (iota((TOK_DEV, TOK_DEV), 0) <= iota((TOK_DEV, TOK_DEV), 1)).astype(bf16)
    count = mm(named[:WIN].astype(bf16), upto)
    code = jnp.where(named[:WIN] > 0.0, count, 0.0).astype(bf16)
    spread = ((iota((ROWS, WIN), 0) >> 3) == iota((ROWS, WIN), 1)).astype(bf16)
    row = iota((ROWS, TOK_DEV), 0)
    codes = mm(spread, code).astype(i32)
    whole = codes == (row & 7) + 1
    late = codes == (row & 3) + (WHOLE + 1)
    second = (row & 4) == 4
    place_ref[...] = whole.astype(bf16)
    for half in range(2):
        cols = slice(half * TOK_DEV, (half + 1) * TOK_DEV)
        late_ref[:, cols] = (late & (second == (half == 1))).astype(bf16)
    for part, out, late_out in zip(split2(weight[:WIN]), parts_refs, late_parts_refs):
        spreads = mm(spread, part)
        out[...] = jnp.where(whole, spreads, 0.0).T.astype(bf16)
        for half in range(2):
            mine = late & (second == (half == 1))
            late_out[half * TOK_DEV : (half + 1) * TOK_DEV, :] = (
                jnp.where(mine, spreads, 0.0).T.astype(bf16)
            )


def halves(wide):
    return jnp.concatenate([wide[:, :HALF], wide[:, HALF:]], axis=0)


def dispatch_kernel(
    left_ref, right_ref, held_ref, settle_ref, place_ref, late_ref, out_ref, bal_ref
):
    rows = jnp.concatenate([left_ref[...], held_ref[...], right_ref[...]], axis=0)
    balanced = mm(settle_ref[...], rows).astype(bf16)
    bal_ref[...] = balanced
    out_ref[:, :D] = mm(place_ref[...], balanced).astype(bf16)
    out_ref[:, D:] = mm(late_ref[...], halves(balanced)).astype(bf16)


def block_source(dim):
    row = iota((BLOCK, BLOCK), dim)
    return ((row >> 2) & 15) * 8 + (row >> 6) * 4 + (row & 3)


def ffn_kernel(rows_ref, gate_ref, up_ref, down_ref, out_ref, x, hidden):
    ordered = (iota((BLOCK, BLOCK), 1) == block_source(0)).astype(bf16)
    back = (iota((BLOCK, BLOCK), 0) == block_source(1)).astype(bf16)
    part_rows = BLOCK // 2
    x[:ROWS, :] = rows_ref[:, :D]
    for b in range(ROWS // BLOCK):
        y = mm(ordered, rows_ref[b * BLOCK : (b + 1) * BLOCK, D:]).astype(bf16)
        mine = slice(ROWS + b * part_rows, ROWS + (b + 1) * part_rows)
        x[mine, :HALF] = y[:part_rows]
        x[mine, HALF:] = y[part_rows:]
    for f in range(FF // FF_CHUNK):
        cols = slice(f * FF_CHUNK, (f + 1) * FF_CHUNK)
        g = mm(x[...], gate_ref[0, :, cols])
        u = mm(x[...], up_ref[0, :, cols])
        hidden[:, cols] = (g / (1.0 + jnp.exp(-g)) * u).astype(bf16)
    late = []
    for half in range(2):
        cols = slice(half * HALF, (half + 1) * HALF)
        y = mm(hidden[...], down_ref[0, :, cols]).astype(bf16)
        out_ref[:, cols] = y[:ROWS]
        late.append(y[ROWS:])
    for b in range(ROWS // BLOCK):
        mine = slice(b * part_rows, (b + 1) * part_rows)
        y = jnp.concatenate([late[0][mine], late[1][mine]], axis=0)
        out_ref[b * BLOCK : (b + 1) * BLOCK, D:] = mm(back, y).astype(bf16)


def against(a, b):
    return lax.dot_general(a, b, (((1,), (1,)), ((), ())), preferred_element_type=f32)


def terms_kernel(
    rows_ref,
    grad_ref,
    bal_ref,
    order_ref,
    place_ref,
    late_ref,
    weight_ref,
    other_ref,
    factor_ref,
):
    cotangent = grad_ref[...]
    scores = against(rows_ref[:, :D], cotangent) * place_ref[...].astype(f32)
    late = against(rows_ref[:, D:], halves(cotangent)) * late_ref[...].astype(f32)
    scores = scores + late[:, :TOK_DEV] + late[:, TOK_DEV:]
    score = jnp.sum(scores.reshape(WIN, WHOLE, TOK_DEV), axis=1)
    weight = weight_ref[...]
    total = jnp.sum(weight[:WIN] * score, axis=0, keepdims=True)
    grad = jnp.concatenate(
        [weight[:WIN] * (score - total), weight[WIN:] * (0.0 - total)], axis=0
    )
    high, low = split2(grad)
    factor = jnp.concatenate(
        [mm(order_ref[...], high).astype(bf16), mm(order_ref[...], low).astype(bf16)], axis=1
    )
    factor_ref[...] = factor[:EXPERTS]
    for half in range(2):
        other_ref[half * EXPERTS : (half + 1) * EXPERTS, :] = half_terms(
            factor[EXPERTS:], bal_ref, half
        ).astype(bf16)


def half_terms(factor, bal_ref, half):
    tokens = bal_ref[:, half * HALF : (half + 1) * HALF]
    term = mm(factor, jnp.concatenate([tokens, tokens], axis=0))
    first = (iota((EXPERTS, QUARTER), 0) & 4) == 0
    return jnp.where(first, term[:, :QUARTER], term[:, QUARTER:])


def join_kernel(factor_ref, bal_ref, given_ref, out_ref):
    for half in range(2):
        rows = slice(half * EXPERTS, (half + 1) * EXPERTS)
        own = half_terms(factor_ref[...], bal_ref, half)
        out_ref[rows, :] = (own + given_ref[rows, :].astype(f32)).astype(bf16)


def output_kernel(
    rows_ref,
    high_ref,
    low_ref,
    late_high_ref,
    late_low_ref,
    factor_ref,
    out_ref,
    handed_ref,
):
    handed_ref[...] = factor_ref[...]
    rows, ends = rows_ref[:, :D], rows_ref[:, D:]
    late = mm(late_high_ref[...], ends) + mm(late_low_ref[...], ends)
    both = mm(high_ref[...], rows) + mm(low_ref[...], rows)
    out_ref[:, :HALF] = (both[:, :HALF] + late[:TOK_DEV]).astype(bf16)
    out_ref[:, HALF:] = (both[:, HALF:] + late[TOK_DEV:]).astype(bf16)


def part_kernel(terms_ref, out_ref):
    part = jnp.sum(terms_ref[...].astype(f32).reshape(2 * CHIPS, 8, QUARTER), axis=0)
    two = jnp.concatenate([part, part], axis=0).astype(bf16)
    for i in range(12):
        out_ref[16 * i : 16 * (i + 1), :] = two


def last_kernel(parts_ref, out_ref):
    parts = jnp.sum(parts_ref[...].astype(f32).reshape(2, 12, 8, QUARTER), axis=1)
    for half in range(2):
        for quarter in range(2):
            at = half * HALF + quarter * QUARTER
            out_ref[:, at : at + QUARTER] = parts[half, 4 * quarter : 4 * quarter + 4]


def in_hbm(array):
    return pltpu.with_memory_space_constraint(array, pltpu.HBM)


def shape(dims, dtype):
    return jax.ShapeDtypeStruct(dims, dtype)


def exchange(blocks, axes, peers, groups=None):
    rows, cols = blocks.shape
    apart = blocks.reshape(peers, rows // peers, cols)
    return lax.all_to_all(
        apart, axes, split_axis=0, concat_axis=0, axis_index_groups=groups, tiled=True
    ).reshape(rows, cols)


def expert_groups():
    return [
        [
            (((side ^ (chip >= CHIPS // 2)) * 12 + z) * CHIPS + chip) * 2 + core
            for chip in range(CHIPS)
            for core in range(2)
        ]
        for z in range(12)
        for side in range(2)
    ]


def borders(rank, core, flows, rollout, ids, logits):
    return call(
        border_kernel,
        [
            shape((MOVE, D), bf16),
            shape((MOVE, D), bf16),
            shape((SRC_DEV, D), bf16),
            shape((TOK_DEV, SPAN), bf16),
            shape((2 * EXPERTS, EXPERTS), bf16),
            shape((ROWS, TOK_DEV), bf16),
            shape((ROWS, 2 * TOK_DEV), bf16),
            shape((EXPERTS, TOK_DEV), f32),
            shape((TOK_DEV, ROWS), bf16),
            shape((TOK_DEV, ROWS), bf16),
            shape((2 * TOK_DEV, ROWS), bf16),
            shape((2 * TOK_DEV, ROWS), bf16),
        ],
        [SMEM] * 2 + [HBM] * 4,
        25_000_000,
        [
            pltpu.SMEM((1, 24), i32),
            pltpu.VMEM((TOPK, TOK_DEV), i32),
            pltpu.VMEM((TOPK, TOK_DEV), f32),
            pltpu.SemaphoreType.DMA((4,)),
        ],
    )(rank, core, *[in_hbm(v) for v in (flows, rollout, ids, logits)])


def dispatch(left, right, held, settle, place, late):
    return call(
        dispatch_kernel,
        [shape((ROWS, WIDTH), bf16), shape((TOK_DEV, D), bf16)],
        [VMEM] * 6,
        12_000_000_000,
    )(left, right, held, settle, place, late)


def ffn(rows, w_gate, w_up, w_down):
    return call(
        ffn_kernel,
        shape((ROWS, WIDTH), bf16),
        [VMEM] * 4,
        3_700_000_000,
        [pltpu.VMEM((SLOTS, D), bf16), pltpu.VMEM((SLOTS, FF), bf16)],
    )(rows, w_gate, w_up, w_down)


def router_terms(rows, grad_out, balanced, order, place, late, weight):
    return call(
        terms_kernel,
        [shape((2 * EXPERTS, QUARTER), bf16), shape((EXPERTS, 2 * TOK_DEV), bf16)],
        [VMEM] * 7,
        500_000_000,
    )(rows, grad_out, balanced, order, place, late, weight)


def join(factor, balanced, given):
    return call(join_kernel, shape((2 * EXPERTS, QUARTER), bf16), [VMEM] * 3, 150_000_000)(
        factor, balanced, given
    )


def layer_output(rows, shares, factor):
    return call(
        output_kernel,
        [shape((TOK_DEV, D), bf16), shape((EXPERTS, 2 * TOK_DEV), bf16)],
        [VMEM] * 6,
        4_000_000_000,
    )(rows, *shares, factor)


def partial_sum(terms):
    return call(part_kernel, shape((192, QUARTER), bf16), [VMEM], 1_000_000)(terms)


def last_sum(parts):
    return call(last_kernel, shape((4, D), f32), [VMEM], 1_000_000)(parts)


def shards(rollout, flows, route_ids, route_logits, grad_out, w_gate, w_up, w_down):
    ranks = lax.axis_size(DP)
    rank = lax.axis_index(DP).reshape(1)
    core = lax.axis_index("core").reshape(1)
    flows = flows.T
    head, tail, held, settle, order, place, late, weight, *shares = borders(
        rank, core, flows, rollout, route_ids.T, route_logits.T
    )
    left = lax.ppermute(tail, DP, [(i, (i + 1) % ranks) for i in range(ranks)])
    right = lax.ppermute(head, DP, [((i + 1) % ranks, i) for i in range(ranks)])
    outgoing, balanced = dispatch(left, right, held, settle, place, late)
    rows = exchange(outgoing, DP + FSDP, WIN, expert_groups())
    computed = ffn(rows, w_gate, w_up, w_down)
    returned = exchange(computed, DP + FSDP, WIN, expert_groups())
    other, factor = router_terms(returned, grad_out, balanced, order, place, late, weight)
    given = lax.ppermute(other, "core", [(0, 1), (1, 0)])
    layer_out, factor = layer_output(returned, shares, factor)
    terms = exchange(join(factor, balanced, given), ("yl", "chip"), 2 * CHIPS)
    parts = exchange(partial_sum(terms), DP, 24)
    return (layer_out, last_sum(parts))


def solution(mesh):
    fine = Mesh(mesh.devices.reshape(2, 12, CHIPS, 2), DP + FSDP)
    rows = P(DP + FSDP, None)
    expert = P(FSDP, None, None)
    return jax.shard_map(
        shards,
        mesh=fine,
        in_specs=(rows, P(None, FSDP), rows, rows, rows, expert, expert, expert),
        out_specs=(rows, P(FSDP, None)),
        check_vma=False,
    )
```
